32 devices in a mesh: beh: 4 (over y, x), node: 8 (over z, core).
Axes of the slice: x: 2, y: 2, z: 4, core: 2. Of those that a mesh axis runs over, the one named last changes fastest.
Arguments:
- embeddings: bfloat16 [16384, 128], P('node'), may hold values from -16 to 16, as said below
- adjacency: bfloat16 [4, 896, 128, 128], P('beh', 'node'), may hold values from -0.1875 to 0.1875
- tile_rows: int32 [4, 896], P('beh', 'node'), may hold values from 0 to 15
- tile_cols: int32 [4, 896], P('beh', 'node'), may hold values from 0 to 3
- tile_count: int32 [4, 8], P('beh', 'node'), may hold values from 28 to 112, as said below
- need_ids: int32 [4, 32], P('beh', 'node'), may hold values from 0 to 127, as said below
- w_query: bfloat16 [128, 128], replicated, may hold values from -0.5 to 0.5
- w_key: bfloat16 [128, 128], replicated, may hold values from -0.5 to 0.5
- w_value: bfloat16 [128, 128], replicated, may hold values from -0.5 to 0.5
- w_out: bfloat16 [128, 128], replicated, may hold values from -0.5 to 0.5
- mlp_gain: float32 [128], replicated, may hold values from 0.1 to 1.9
- w_up: bfloat16 [128, 512], replicated, may hold values from -0.5 to 0.5
- w_down: bfloat16 [512, 128], replicated, may hold values from -0.25 to 0.25
Outputs:
- merged: bfloat16 [4, 16384, 128], P('beh', 'node')
The draws below stay inside these ranges and needn't reach their ends.
Inputs may be any that keep to these rules, and one draw needn't show every extreme that they name: `tile_count`: live slots of one behavior and shard; every behavior has a shard with all 112 slots live. `need_ids`: for each behavior b and shard n, entry n * 4 + m (m < 4) names a block owned by shard 2 m or shard 2 m + 1, block g being owned by shard g // 16. `embeddings`: entries keep within the stated bound.
All inputs are finite; a program needn't handle non-finite values.
Results may differ from the reference program's by a relative error of at most 0.0077.
Values may be sent and summed in bfloat16 or wider, within the bound.
No kernel may reach another device: no remote copies, remote signals or barrier semaphores. Data moves between devices by JAX's collectives and lax.ppermute only.
A program may use at most 64 MiB of HBM per device.

```python
import math
import jax
import jax.numpy as jnp
from jax import lax

D = 128
TB = 128
HEADS = 4
HEAD = 32
FF = 512
NODE_DEV = 2048
TILE_DEV = 112
BLK_DEV = 16
NEED = 4
NODES = 16384
N_BEH = 4
N_NODE = 8


def draw_embeddings(key, part):
    base_key = jax.random.fold_in(key, 11)
    entries = jax.random.normal(base_key, (NODES, D), jnp.float32)
    return jnp.clip(entries, -6.0, 6.0).astype(jnp.bfloat16)


def draw_tile_count(key, part):
    counts = jax.random.randint(jax.random.fold_in(key, 21), (N_BEH, N_NODE), TILE_DEV // 4, TILE_DEV + 1)
    where_full = jax.random.randint(jax.random.fold_in(key, 22), (N_BEH,), 0, N_NODE)
    columns = jnp.arange(N_NODE, dtype=jnp.int32)[None, :]
    return jnp.where(columns == where_full[:, None], TILE_DEV, counts).astype(jnp.int32)


def draw_need_ids(key, part):
    parity = jax.random.randint(jax.random.fold_in(key, 31), (N_BEH, N_NODE, NEED), 0, 2)
    owners = 2 * jnp.arange(NEED, dtype=jnp.int32)[None, None, :] + parity
    within = jax.random.randint(jax.random.fold_in(key, 32), (N_BEH, N_NODE, NEED), 0, BLK_DEV)
    return (owners * BLK_DEV + within).reshape(N_BEH, N_NODE * NEED).astype(jnp.int32)


def plant(values, stream_key, least, top_value):
    longest = values.shape.index(max(values.shape))
    spots = []
    for shift in (0, 1):
        where = [jax.random.randint(jax.random.fold_in(stream_key, axis), (), 0, length) for axis, length in enumerate(values.shape)]
        where[longest] = (where[longest] + shift) % values.shape[longest]
        spots.append(tuple(where))
    return values.at[spots[0]].set(least).at[spots[1]].set(top_value)


def levels(stream_key, shape, cuts, smallest, top_value):
    factor_of = 1.0
    for axis_at, blocks in cuts:
        heights = jax.random.uniform(jax.random.fold_in(jax.random.fold_in(stream_key, 6), axis_at), (blocks,), jnp.float32, smallest / len(cuts), top_value / len(cuts))
        factor_of = factor_of * jnp.repeat(jnp.exp(heights), shape[axis_at] // blocks).reshape((-1,) + (1,) * (len(shape) - 1 - axis_at))
    return factor_of


def gaussian(stream_key, shape, deviation, limit, cuts=(), held_as=jnp.bfloat16):
    values = deviation * jax.random.normal(stream_key, shape, jnp.float32)
    if cuts:
        values = values * levels(stream_key, shape, cuts, -0.22, 0.18)
    return jnp.clip(values, -limit, limit).astype(held_as)


def setup_inputs(seed: int = 0) -> dict:
    key_of = jax.random.split(jax.random.key(seed), 14)
    return {
        "embeddings": draw_embeddings(jax.random.fold_in(key_of[13], 71), 0),
        "adjacency": gaussian(key_of[1], (N_BEH, N_NODE * TILE_DEV, TB, TB), (TB * TILE_DEV // BLK_DEV) ** -0.5, 0.1875, ((0, 4), (1, 8))),
        "tile_rows": plant(jax.random.randint(key_of[2], (N_BEH, N_NODE * TILE_DEV), 0, BLK_DEV), jax.random.fold_in(key_of[2], 1), 0, BLK_DEV - 1).astype(jnp.int32),
        "tile_cols": plant(jax.random.randint(key_of[3], (N_BEH, N_NODE * TILE_DEV), 0, NEED), jax.random.fold_in(key_of[3], 1), 0, NEED - 1).astype(jnp.int32),
        "tile_count": draw_tile_count(jax.random.fold_in(key_of[13], 71), 0),
        "need_ids": draw_need_ids(jax.random.fold_in(key_of[13], 71), 0),
        "w_query": gaussian(key_of[6], (D, D), D ** -0.5, 0.5),
        "w_key": gaussian(key_of[7], (D, D), D ** -0.5, 0.5),
        "w_value": gaussian(key_of[8], (D, D), D ** -0.5, 0.5),
        "w_out": gaussian(key_of[9], (D, D), D ** -0.5, 0.5),
        "mlp_gain": jnp.clip(1.0 + 0.18 * jax.random.normal(key_of[10], (D,), jnp.float32), 0.1, 1.9),
        "w_up": gaussian(key_of[11], (D, FF), D ** -0.5, 0.5),
        "w_down": gaussian(key_of[12], (FF, D), FF ** -0.5, 0.25),
    }


def merge_behaviors(behaviors, queries, w_query, w_key, w_value, w_out, mlp_gain, w_up, w_down):
    count_k, row_count, feature = behaviors.shape
    count_q = queries.shape[0]
    flat_keys = behaviors.reshape(count_k * row_count, feature)
    key_rows = jnp.dot(flat_keys, w_key, preferred_element_type=jnp.float32).reshape(count_k, row_count, HEADS, HEAD)
    value_rows = jnp.dot(flat_keys, w_value, preferred_element_type=jnp.float32).reshape(count_k, row_count, HEADS, HEAD)
    flat_queries = queries.reshape(count_q * row_count, feature)
    query_rows = jnp.dot(flat_queries, w_query, preferred_element_type=jnp.float32).reshape(count_q, row_count, HEADS, HEAD)
    scores = jnp.einsum('qrhe,krhe->qrhk', query_rows, key_rows, precision=lax.Precision.HIGHEST) / math.sqrt(HEAD)
    highest = lax.optimization_barrier(jnp.max(scores, axis=-1, keepdims=True))
    weights = jnp.exp(scores - highest)
    weights = weights / lax.optimization_barrier(jnp.sum(weights, axis=-1, keepdims=True))
    mixture = jnp.einsum('qrhk,krhe->qrhe', weights, value_rows, precision=lax.Precision.HIGHEST)
    mixture = mixture.reshape(count_q * row_count, feature).astype(jnp.bfloat16)
    residual = flat_queries.astype(jnp.float32) + jnp.dot(mixture, w_out, preferred_element_type=jnp.float32)
    meansq = lax.optimization_barrier(jnp.mean(residual * residual, axis=-1, keepdims=True))
    normed = (residual * lax.rsqrt(meansq + 1e-06) * mlp_gain.astype(jnp.float32)).astype(jnp.bfloat16)
    hidden = jax.nn.silu(jnp.dot(normed, w_up, preferred_element_type=jnp.float32)).astype(jnp.bfloat16)
    result = residual + jnp.dot(hidden, w_down, preferred_element_type=jnp.float32)
    return result.astype(jnp.bfloat16).reshape(count_q, row_count, feature)

def reference(embeddings, adjacency, tile_rows, tile_cols, tile_count, need_ids, w_query, w_key, w_value, w_out, mlp_gain, w_up, w_down):
    block_total = NODES // TB
    blocks = embeddings.reshape(block_total, TB, D)
    shards = N_BEH * N_NODE
    flat_tiles = adjacency.reshape(shards, TILE_DEV, TB, TB)
    flat_rows = tile_rows.reshape(shards, TILE_DEV)
    flat_cols = tile_cols.reshape(shards, TILE_DEV)
    flat_count = tile_count.reshape(shards)
    flat_need = need_ids.reshape(shards, NEED)
    shard_ids = jnp.arange(shards, dtype=jnp.int32) % N_NODE

    def propagate(pieces):
        tile_block, row_block, col_index, count_now, needed, shard_id = pieces
        sources = blocks[needed[col_index]].astype(jnp.float32)
        product = jnp.einsum('tij,tjd->tid', tile_block.astype(jnp.float32), sources, precision=lax.Precision.HIGHEST)
        active = jnp.arange(TILE_DEV, dtype=jnp.int32) < count_now
        select = ((row_block[:, None] == jnp.arange(BLK_DEV, dtype=jnp.int32)[None, :]) & active[:, None]).astype(jnp.float32)
        summed = jnp.einsum('tb,tid->bid', select, product, precision=lax.Precision.HIGHEST).reshape(NODE_DEV, D)
        start = (shard_id * NODE_DEV).astype(jnp.int32)
        own_rows = lax.dynamic_slice_in_dim(embeddings, start, NODE_DEV, 0)
        return (summed + own_rows.astype(jnp.float32)).astype(jnp.bfloat16)
    spread = lax.map(propagate, (flat_tiles, flat_rows, flat_cols, flat_count, flat_need, shard_ids))
    spread = spread.reshape(N_BEH, N_NODE, NODE_DEV, D)

    def merge_shard(group_rows):
        return merge_behaviors(group_rows, group_rows, w_query, w_key, w_value, w_out, mlp_gain, w_up, w_down)
    merged_all = lax.map(merge_shard, jnp.transpose(spread, (1, 0, 2, 3)))
    return jnp.transpose(merged_all, (1, 0, 2, 3)).reshape(N_BEH, NODES, D)
```

```python
import functools
import math

import jax
import jax.numpy as jnp
from jax import lax
from jax.experimental import pallas as pl
from jax.experimental.pallas import tpu as pltpu
from jax.sharding import PartitionSpec as P

TB = 128
HEADS = 4
HEAD = 32
F32 = jnp.float32
BF16 = jnp.bfloat16
SMEM = pl.BlockSpec(memory_space=pltpu.SMEM)
VMEM = pl.BlockSpec(memory_space=pltpu.VMEM)
ANY = pl.BlockSpec(memory_space=pl.ANY)
VMEM_LIMIT = 48 * 2**20


def exchange(value, axis, mask):
    pairs = [(source, source ^ mask) for source in range(lax.axis_size(axis))]
    return lax.ppermute(value, axis, pairs)


def params(**more):
    return pltpu.CompilerParams(vmem_limit_bytes=VMEM_LIMIT, **more)


def cost(flops, moved):
    return pl.CostEstimate(flops=flops, bytes_accessed=moved, transcendentals=0)


def cells_kernel(chunk, pairs, cell_count, place, rows, cols, count, tiles, out, total):
    step = pl.program_id(0)

    @pl.when(step == 0)
    def _():
        total[...] = jnp.zeros_like(total)

    for i in range(chunk):
        slot = step * chunk + i
        cell = rows[0, slot] * pairs + (cols[0, slot] ^ place[0])
        cell = jnp.where(slot < count[0, 0], cell, cell_count)
        total[cell] += tiles[i].astype(F32)

    @pl.when(step == pl.num_programs(0) - 1)
    def _():
        out[...] = total[:cell_count].astype(BF16)


def sum_cells(place, rows, cols, count, tiles, pairs, block_count):
    slots = tiles.shape[0]
    chunk = math.gcd(slots, 16)
    cell_count = pairs * block_count
    return pl.pallas_call(
        functools.partial(cells_kernel, chunk, pairs, cell_count),
        grid=(slots // chunk,),
        in_specs=[SMEM] * 4 + [pl.BlockSpec((chunk, TB, TB), lambda s: (s, 0, 0))],
        out_specs=pl.BlockSpec((cell_count, TB, TB), lambda s: (0, 0, 0)),
        out_shape=jax.ShapeDtypeStruct((cell_count, TB, TB), BF16),
        scratch_shapes=[pltpu.VMEM((cell_count + 1, TB, TB), F32)],
        compiler_params=params(),
        cost_estimate=cost(0, tiles.size * 2),
        name="cells",
    )(place, rows, cols, count, tiles)


def serve_kernel(block_count, pairs, place, *refs):
    asks, (own, other), outs, sems = refs[:pairs], refs[pairs : pairs + 2], refs[pairs + 2 : -1], refs[-1]
    here, core = place[0], place[1]
    for phase in (0, 1):
        for k in range(pairs):
            block = asks[k][0, here] - 2 * here * block_count
            upper = (block >= block_count).astype(jnp.int32)
            start = pl.multiple_of((block - upper * block_count) * TB, TB)
            for source, match in ((own, upper == core), (other, upper != core)):

                @pl.when(match)
                def _():
                    copy = pltpu.make_async_copy(source.at[pl.ds(start, TB), :], outs[k], sems.at[k])
                    if phase == 0:
                        copy.start()
                    else:
                        copy.wait()


def serve(place, asks, own, other, block_count):
    pairs = len(asks)
    return pl.pallas_call(
        functools.partial(serve_kernel, block_count, pairs),
        in_specs=[SMEM] * (1 + pairs) + [ANY] * 2,
        out_specs=[ANY] * pairs,
        out_shape=[jax.ShapeDtypeStruct((TB, own.shape[1]), own.dtype)] * pairs,
        scratch_shapes=[pltpu.SemaphoreType.DMA((pairs,))],
        name="serve",
    )(place, *asks, own, other)


def spread_kernel(pairs, order, cells, *refs):
    sources, own, outs = refs[:pairs], refs[pairs], refs[pairs + 1 :]
    feature = own.shape[1]
    stack = jnp.concatenate([s[...] for s in sources], axis=0)
    size = outs[0].shape[0]
    for k, out in enumerate(outs):
        start = pl.multiple_of(order[k] * size, size)
        block = order[k] * (size // TB)
        for r in range(size // TB):
            lhs = jnp.concatenate([cells[(block + r) * pairs + m] for m in range(pairs)], axis=1)
            part = jnp.dot(lhs, stack, preferred_element_type=F32)
            rows = own[pl.ds(start + r * TB, TB), :].astype(F32)
            out[r * TB : (r + 1) * TB, :] = (part + rows).astype(BF16)


def spread_cells(order, cells, sources, own, parts):
    size = own.shape[0] // parts
    return pl.pallas_call(
        functools.partial(spread_kernel, len(sources)),
        in_specs=[SMEM] + [VMEM] * (len(sources) + 2),
        out_specs=[VMEM] * parts,
        out_shape=[jax.ShapeDtypeStruct((size, own.shape[1]), BF16)] * parts,
        compiler_params=params(),
        name="spread",
    )(order, cells, *sources, own)


def merge_kernel(count, tile, *refs):
    xs = refs[:count]
    w_qkv, w_out, gain, w_up, w_down = refs[count : count + 5]
    outs = refs[count + 5 :]
    feature = w_out.shape[0]
    scale = math.log2(math.e) / math.sqrt(HEAD)

    def body(step, carry):
        start = pl.multiple_of(step * tile, tile)
        rows = pl.ds(start, tile)
        queries, keys, values = [], [], []
        for x in xs:
            full = lax.dot_general(
                w_qkv[...], x[rows, :], (((1,), (1,)), ((), ())), preferred_element_type=F32
            )
            queries.append(full[:feature].reshape(HEADS, HEAD, tile) * scale)
            keys.append(full[feature : 2 * feature].reshape(HEADS, HEAD, tile))
            values.append(full[2 * feature :].reshape(HEADS, HEAD, tile))
        for x, query, out in zip(xs, queries, outs):
            scores = [jnp.sum(query * key, axis=1, keepdims=True) for key in keys]
            top = functools.reduce(jnp.maximum, scores)
            weights = [jnp.exp2(s - top) for s in scores]
            inverse = 1.0 / functools.reduce(jnp.add, weights)
            mixture = functools.reduce(
                jnp.add, [(w * inverse) * value for w, value in zip(weights, values)]
            )
            mixture = mixture.reshape(feature, tile).astype(BF16)
            residual = x[rows, :].astype(F32) + lax.dot_general(
                mixture, w_out[...], (((0,), (0,)), ((), ())), preferred_element_type=F32
            )
            meansq = jnp.mean(residual * residual, axis=-1, keepdims=True)
            normed = (residual * lax.rsqrt(meansq + 1e-06) * gain[...]).astype(BF16)
            half = 0.5 * jnp.dot(normed, w_up[...], preferred_element_type=F32)
            hidden = (half + half * jnp.tanh(half)).astype(BF16)
            result = residual + jnp.dot(hidden, w_down[...], preferred_element_type=F32)
            out[rows, :] = result.astype(BF16)
        return carry

    lax.fori_loop(0, xs[0].shape[0] // tile, body, 0)


def merge(xs, w_qkv, w_out, gain, w_up, w_down):
    size, feature = xs[0].shape
    tile = math.gcd(size, 256)
    return pl.pallas_call(
        functools.partial(merge_kernel, len(xs), tile),
        in_specs=[VMEM] * (len(xs) + 5),
        out_specs=[VMEM] * len(xs),
        out_shape=[jax.ShapeDtypeStruct((size, feature), BF16)] * len(xs),
        compiler_params=params(),
        name="merge",
    )(*xs, w_qkv, w_out, gain, w_up, w_down)


def place_kernel(order, *refs):
    parts, out, sems = refs[:-2], refs[-2], refs[-1]
    size = parts[0].shape[0]
    copies = []
    for k, part in enumerate(parts):
        start = pl.multiple_of(order[k] * size, size)
        copies.append(pltpu.make_async_copy(part, out.at[pl.ds(start, size), :], sems.at[k]))
        copies[-1].start()
    for copy in copies:
        copy.wait()


def place_parts(order, parts):
    size, feature = parts[0].shape
    return pl.pallas_call(
        place_kernel,
        in_specs=[SMEM] + [ANY] * len(parts),
        out_specs=ANY,
        out_shape=jax.ShapeDtypeStruct((size * len(parts), feature), BF16),
        scratch_shapes=[pltpu.SemaphoreType.DMA((len(parts),))],
        name="place",
    )(order, *parts)


def tiles_kernel(chunk, rows, cols, count, tiles, sources, own, out, total):
    step = pl.program_id(0)

    @pl.when(step == 0)
    def _():
        total[...] = own[...].astype(F32)

    for i in range(chunk):
        slot = step * chunk + i

        @pl.when(slot < count[0, 0])
        def _():
            start = pl.multiple_of(rows[0, slot] * TB, TB)
            total[pl.ds(start, TB), :] += jnp.dot(
                tiles[i], sources[cols[0, slot]], preferred_element_type=F32
            )

    @pl.when(step == pl.num_programs(0) - 1)
    def _():
        out[...] = total[...].astype(BF16)


def spread_tiles(rows, cols, count, tiles, sources, own):
    slots = tiles.shape[0]
    chunk = math.gcd(slots, 16)
    return pl.pallas_call(
        functools.partial(tiles_kernel, chunk),
        grid=(slots // chunk,),
        in_specs=[SMEM] * 3
        + [
            pl.BlockSpec((chunk, TB, TB), lambda s: (s, 0, 0)),
            pl.BlockSpec(sources.shape, lambda s: (0, 0, 0)),
            pl.BlockSpec(own.shape, lambda s: (0, 0)),
        ],
        out_specs=pl.BlockSpec(own.shape, lambda s: (0, 0)),
        out_shape=jax.ShapeDtypeStruct(own.shape, BF16),
        scratch_shapes=[pltpu.VMEM(own.shape, F32)],
        compiler_params=params(),
        name="tiles",
    )(rows, cols, count, tiles, sources, own)


def fetch_many(embeddings, need_ids, block_count):
    peer_count = lax.axis_size("node")
    feature = embeddings.shape[1]
    needed = need_ids[0]
    owners = needed // block_count
    within = needed % block_count
    peer_ids = jnp.arange(peer_count, dtype=jnp.int32)
    matches = owners[:, None] == peer_ids[None, :]
    request = jnp.sum(jnp.where(matches, within[:, None] + 1, 0), axis=0)
    swapped = request.reshape(-1, 2)[:, ::-1].reshape(-1)
    request_pair = jnp.stack([request, swapped], axis=1)
    incoming = lax.all_to_all(request_pair, "node", split_axis=0, concat_axis=0, tiled=True)
    parity = lax.axis_index("node") % 2
    own = embeddings.reshape(block_count, TB, feature)
    other = exchange(embeddings, "node", 1).reshape(block_count, TB, feature)
    stack = jnp.concatenate([own, other], axis=0)
    codes = jnp.where(incoming[:, 0] > 0, incoming[:, 0], block_count + incoming[:, 1])
    half = TB // 2
    halves = lax.dynamic_slice_in_dim(stack, parity * half, half, 1)
    chooser = (codes[:, None] - 1 == jnp.arange(2 * block_count, dtype=jnp.int32)[None, :]).astype(BF16)
    outgoing = jnp.einsum("pk,kid->pid", chooser, halves, preferred_element_type=F32).astype(BF16)
    arrived = lax.all_to_all(outgoing, "node", split_axis=0, concat_axis=0, tiled=True)
    return arrived.reshape(peer_count // 2, TB, feature)


def shards(
    embeddings,
    adjacency,
    tile_rows,
    tile_cols,
    tile_count,
    need_ids,
    w_query,
    w_key,
    w_value,
    w_out,
    mlp_gain,
    w_up,
    w_down,
):
    parts = lax.axis_size("beh")
    pairs = lax.axis_size("node") // 2
    block_count = embeddings.shape[0] // TB
    tiles = adjacency[0]
    me = lax.axis_index("beh")
    here = lax.axis_index("node")
    order = jnp.stack([me ^ k for k in range(parts)]).astype(jnp.int32)
    if pairs * block_count <= tiles.shape[0]:
        place = jnp.stack([here // 2, here % 2]).astype(jnp.int32)
        asks = [need_ids] + [exchange(need_ids, "node", 2 * k) for k in range(1, pairs)]
        other = exchange(embeddings, "node", 1)
        cells = sum_cells(place, tile_rows, tile_cols, tile_count, tiles, pairs, block_count)
        served = serve(place, asks, embeddings, other, block_count)
        sources = [served[0]] + [exchange(served[k], "node", 2 * k) for k in range(1, pairs)]
        quarters = spread_cells(order, cells, sources, embeddings, parts)
    else:
        sources = fetch_many(embeddings, need_ids, block_count)
        spread = spread_tiles(tile_rows, tile_cols, tile_count, tiles, sources, embeddings)
        size = spread.shape[0] // parts
        quarters = [lax.dynamic_slice_in_dim(spread, order[k] * size, size, 0) for k in range(parts)]
    xs = [quarters[0]] + [exchange(quarters[k], "beh", k) for k in range(1, parts)]
    w_qkv = jnp.concatenate([w_query, w_key, w_value], axis=1).T
    merged = merge(xs, w_qkv, w_out, mlp_gain[None], w_up, w_down)
    back = [merged[0]] + [exchange(merged[k], "beh", k) for k in range(1, parts)]
    return place_parts(order, back)[None]


def solution(mesh):
    in_specs = (
        P("node", None),
        P("beh", "node", None, None),
        P("beh", "node"),
        P("beh", "node"),
        P("beh", "node"),
        P("beh", "node"),
        P(),
        P(),
        P(),
        P(),
        P(),
        P(),
        P(),
    )
    out_specs = P("beh", "node", None)
    return jax.shard_map(shards, mesh=mesh, in_specs=in_specs, out_specs=out_specs, check_vma=False)
```

```python
import functools
import math

import jax
import jax.numpy as jnp
from jax import lax
from jax.experimental import pallas as pl
from jax.experimental.pallas import tpu as pltpu
from jax.sharding import PartitionSpec as P

TB = 128
HEADS = 4
HEAD = 32
F32 = jnp.float32
BF16 = jnp.bfloat16
SMEM = pl.BlockSpec(memory_space=pltpu.SMEM)
VMEM = pl.BlockSpec(memory_space=pltpu.VMEM)
ANY = pl.BlockSpec(memory_space=pl.ANY)
HBM = pl.BlockSpec(memory_space=pltpu.HBM)
VMEM_LIMIT = 48 * 2**20


def hbm(*values):
    return [pltpu.with_memory_space_constraint(v, pltpu.HBM) for v in values]


def vmem(*values):
    return [pltpu.with_memory_space_constraint(v, pltpu.VMEM) for v in values]


def exchange(value, axis, mask):
    pairs = [(source, source ^ mask) for source in range(lax.axis_size(axis))]
    return lax.ppermute(value, axis, pairs)


def params(**more):
    return pltpu.CompilerParams(vmem_limit_bytes=VMEM_LIMIT, **more)


def cost(flops, moved):
    return pl.CostEstimate(flops=flops, bytes_accessed=moved, transcendentals=0)


def cells_kernel(chunk, pairs, cell_count, *refs):
    rows, cols, count, tiles, out, total, held, row_list, col_list, sems = refs
    steps = tiles.shape[0] // chunk
    here = lax.axis_index("node") // 2
    lists = [
        pltpu.make_async_copy(source, target, sems.at[steps + k])
        for k, (source, target) in enumerate(((rows, row_list), (cols, col_list)))
    ]
    loads = [
        pltpu.make_async_copy(tiles.at[pl.ds(s * chunk, chunk)], held.at[s], sems.at[s]) for s in range(steps)
    ]
    for copy in lists + loads:
        copy.start()
    total[...] = jnp.zeros_like(total)
    for copy in lists:
        copy.wait()
    for step, load in enumerate(loads):
        load.wait()
        for i in range(chunk):
            slot = step * chunk + i
            cell = row_list[0, slot] * pairs + (col_list[0, slot] ^ here)
            cell = jnp.where(slot < count[0, 0], cell, cell_count)
            total[cell] += held[step, i].astype(F32)
    out[...] = total[:cell_count].astype(BF16)


def sum_cells(rows, cols, count, tiles, pairs, block_count):
    slots = tiles.shape[0]
    chunk = math.gcd(slots, 16)
    cell_count = pairs * block_count
    return pl.pallas_call(
        functools.partial(cells_kernel, chunk, pairs, cell_count),
        in_specs=[HBM, HBM, SMEM, HBM],
        out_specs=VMEM,
        out_shape=jax.ShapeDtypeStruct((cell_count, TB, TB), BF16),
        scratch_shapes=[
            pltpu.VMEM((cell_count + 1, TB, TB), F32),
            pltpu.VMEM((slots // chunk, chunk, TB, TB), BF16),
            pltpu.SMEM(rows.shape, jnp.int32),
            pltpu.SMEM(cols.shape, jnp.int32),
            pltpu.SemaphoreType.DMA((slots // chunk + 2,)),
        ],
        compiler_params=params(),
        cost_estimate=cost(0, tiles.size * 2),
        name="cells",
    )(*hbm(rows, cols), count, *hbm(tiles))


def serve_kernel(block_count, pairs, *refs):
    asks, (own, other), outs = refs[:pairs], refs[pairs : pairs + 2], refs[pairs + 2 : 2 * pairs + 2]
    lists, sems = refs[2 * pairs + 2 : -1], refs[-1]
    here = lax.axis_index("node") // 2
    core = lax.axis_index("node") % 2
    copies = [
        pltpu.make_async_copy(ask, target, sems.at[k]) for k, (ask, target) in enumerate(zip(asks, lists))
    ]
    for copy in copies:
        copy.start()
    for copy in copies:
        copy.wait()
    for k, out in enumerate(outs):
        block = lists[k][0, here] - 2 * here * block_count
        upper = (block >= block_count).astype(jnp.int32)
        start = pl.multiple_of((block - upper * block_count) * TB, TB)

        @pl.when(upper == core)
        def _():
            out[...] = own[pl.ds(start, TB), :]

        @pl.when(upper != core)
        def _():
            out[...] = other[pl.ds(start, TB), :]


def serve(asks, own, other, block_count):
    pairs = len(asks)
    return pl.pallas_call(
        functools.partial(serve_kernel, block_count, pairs),
        in_specs=[ANY] * pairs + [VMEM] * 2,
        out_specs=[VMEM] * pairs,
        out_shape=[jax.ShapeDtypeStruct((TB, own.shape[1]), own.dtype)] * pairs,
        scratch_shapes=[pltpu.SMEM(asks[0].shape, jnp.int32)] * pairs + [pltpu.SemaphoreType.DMA((pairs,))],
        compiler_params=params(),
        name="serve",
    )(*asks, own, other)


def spread_kernel(pairs, cells, *refs):
    sources, own, outs = refs[:pairs], refs[pairs], refs[pairs + 1 :]
    me = lax.axis_index("beh")
    stack = jnp.concatenate([s[...] for s in sources], axis=0)
    size = outs[0].shape[0]
    for k, out in enumerate(outs):
        start = pl.multiple_of((me ^ k) * size, size)
        block = (me ^ k) * (size // TB)
        for r in range(size // TB):
            lhs = jnp.concatenate([cells[(block + r) * pairs + m] for m in range(pairs)], axis=1)
            part = jnp.dot(lhs, stack, preferred_element_type=F32)
            rows = own[pl.ds(start + r * TB, TB), :].astype(F32)
            out[r * TB : (r + 1) * TB, :] = (part + rows).astype(BF16)


def spread_cells(cells, sources, own, parts):
    size = own.shape[0] // parts
    return pl.pallas_call(
        functools.partial(spread_kernel, len(sources)),
        in_specs=[VMEM] * (len(sources) + 2),
        out_specs=[VMEM] * parts,
        out_shape=[jax.ShapeDtypeStruct((size, own.shape[1]), BF16)] * parts,
        compiler_params=params(),
        name="spread",
    )(cells, *sources, own)


def merge_kernel(count, tile, *refs):
    xs = refs[:count]
    w_qkv, w_out, gain, w_up, w_down = refs[count : count + 5]
    outs = refs[count + 5 :]
    feature = w_out.shape[0]
    scale = math.log2(math.e) / math.sqrt(HEAD)

    def body(step, carry):
        start = pl.multiple_of(step * tile, tile)
        rows = pl.ds(start, tile)
        queries, keys, values = [], [], []
        for x in xs:
            full = lax.dot_general(
                w_qkv[...], x[rows, :], (((1,), (1,)), ((), ())), preferred_element_type=F32
            )
            queries.append(full[:feature].reshape(HEADS, HEAD, tile) * scale)
            keys.append(full[feature : 2 * feature].reshape(HEADS, HEAD, tile))
            values.append(full[2 * feature :].reshape(HEADS, HEAD, tile))
        for x, query, out in zip(xs, queries, outs):
            scores = [jnp.sum(query * key, axis=1, keepdims=True) for key in keys]
            top = functools.reduce(jnp.maximum, scores)
            weights = [jnp.exp2(s - top) for s in scores]
            inverse = 1.0 / functools.reduce(jnp.add, weights)
            mixture = functools.reduce(
                jnp.add, [(w * inverse) * value for w, value in zip(weights, values)]
            )
            mixture = mixture.reshape(feature, tile).astype(BF16)
            residual = x[rows, :].astype(F32) + lax.dot_general(
                mixture, w_out[...], (((0,), (0,)), ((), ())), preferred_element_type=F32
            )
            meansq = jnp.mean(residual * residual, axis=-1, keepdims=True)
            normed = (residual * lax.rsqrt(meansq + 1e-06) * gain[...]).astype(BF16)
            half = 0.5 * jnp.dot(normed, w_up[...], preferred_element_type=F32)
            hidden = (half + half * jnp.tanh(half)).astype(BF16)
            result = residual + jnp.dot(hidden, w_down[...], preferred_element_type=F32)
            out[rows, :] = result.astype(BF16)
        return carry

    lax.fori_loop(0, xs[0].shape[0] // tile, body, 0)


def merge(xs, w_qkv, w_out, gain, w_up, w_down):
    size, feature = xs[0].shape
    tile = math.gcd(size, 256)
    return pl.pallas_call(
        functools.partial(merge_kernel, len(xs), tile),
        in_specs=[VMEM] * (len(xs) + 5),
        out_specs=[VMEM] * len(xs),
        out_shape=[jax.ShapeDtypeStruct((size, feature), BF16)] * len(xs),
        compiler_params=params(),
        name="merge",
    )(*xs, w_qkv, w_out, gain, w_up, w_down)


def place_kernel(*refs):
    me = lax.axis_index("beh")
    parts, out, sems = refs[:-2], refs[-2], refs[-1]
    size = parts[0].shape[0]
    copies = []
    for k, part in enumerate(parts):
        start = pl.multiple_of((me ^ k) * size, size)
        copies.append(pltpu.make_async_copy(part, out.at[pl.ds(start, size), :], sems.at[k]))
        copies[-1].start()
    for copy in copies:
        copy.wait()


def place_parts(parts):
    size, feature = parts[0].shape
    return pl.pallas_call(
        place_kernel,
        in_specs=[VMEM] * len(parts),
        out_specs=HBM,
        out_shape=jax.ShapeDtypeStruct((size * len(parts), feature), BF16),
        scratch_shapes=[pltpu.SemaphoreType.DMA((len(parts),))],
        name="place",
    )(*vmem(*parts))


def tiles_kernel(chunk, rows, cols, count, tiles, sources, own, out, total):
    step = pl.program_id(0)

    @pl.when(step == 0)
    def _():
        total[...] = own[...].astype(F32)

    for i in range(chunk):
        slot = step * chunk + i

        @pl.when(slot < count[0, 0])
        def _():
            start = pl.multiple_of(rows[0, slot] * TB, TB)
            total[pl.ds(start, TB), :] += jnp.dot(
                tiles[i], sources[cols[0, slot]], preferred_element_type=F32
            )

    @pl.when(step == pl.num_programs(0) - 1)
    def _():
        out[...] = total[...].astype(BF16)


def spread_tiles(rows, cols, count, tiles, sources, own):
    slots = tiles.shape[0]
    chunk = math.gcd(slots, 16)
    return pl.pallas_call(
        functools.partial(tiles_kernel, chunk),
        grid=(slots // chunk,),
        in_specs=[SMEM] * 3
        + [
            pl.BlockSpec((chunk, TB, TB), lambda s: (s, 0, 0)),
            pl.BlockSpec(sources.shape, lambda s: (0, 0, 0)),
            pl.BlockSpec(own.shape, lambda s: (0, 0)),
        ],
        out_specs=pl.BlockSpec(own.shape, lambda s: (0, 0)),
        out_shape=jax.ShapeDtypeStruct(own.shape, BF16),
        scratch_shapes=[pltpu.VMEM(own.shape, F32)],
        compiler_params=params(),
        name="tiles",
    )(rows, cols, count, tiles, sources, own)


def fetch_many(embeddings, need_ids, block_count):
    peer_count = lax.axis_size("node")
    feature = embeddings.shape[1]
    needed = need_ids[0]
    owners = needed // block_count
    within = needed % block_count
    peer_ids = jnp.arange(peer_count, dtype=jnp.int32)
    matches = owners[:, None] == peer_ids[None, :]
    request = jnp.sum(jnp.where(matches, within[:, None] + 1, 0), axis=0)
    swapped = request.reshape(-1, 2)[:, ::-1].reshape(-1)
    request_pair = jnp.stack([request, swapped], axis=1)
    incoming = lax.all_to_all(request_pair, "node", split_axis=0, concat_axis=0, tiled=True)
    parity = lax.axis_index("node") % 2
    own = embeddings.reshape(block_count, TB, feature)
    other = exchange(embeddings, "node", 1).reshape(block_count, TB, feature)
    stack = jnp.concatenate([own, other], axis=0)
    codes = jnp.where(incoming[:, 0] > 0, incoming[:, 0], block_count + incoming[:, 1])
    half = TB // 2
    halves = lax.dynamic_slice_in_dim(stack, parity * half, half, 1)
    chooser = (codes[:, None] - 1 == jnp.arange(2 * block_count, dtype=jnp.int32)[None, :]).astype(BF16)
    outgoing = jnp.einsum("pk,kid->pid", chooser, halves, preferred_element_type=F32).astype(BF16)
    arrived = lax.all_to_all(outgoing, "node", split_axis=0, concat_axis=0, tiled=True)
    return arrived.reshape(peer_count // 2, TB, feature)


def shards(
    embeddings,
    adjacency,
    tile_rows,
    tile_cols,
    tile_count,
    need_ids,
    w_query,
    w_key,
    w_value,
    w_out,
    mlp_gain,
    w_up,
    w_down,
):
    parts = lax.axis_size("beh")
    pairs = lax.axis_size("node") // 2
    block_count = embeddings.shape[0] // TB
    tiles = adjacency[0]
    me = lax.axis_index("beh")
    if pairs * block_count <= tiles.shape[0]:
        asks = [need_ids] + [exchange(need_ids, "node", 2 * k) for k in range(1, pairs)]
        other = exchange(embeddings, "node", 1)
        cells = sum_cells(tile_rows, tile_cols, tile_count, tiles, pairs, block_count)
        served = serve(asks, embeddings, other, block_count)
        sources = [served[0]] + [exchange(served[k], "node", 2 * k) for k in range(1, pairs)]
        quarters = spread_cells(cells, sources, embeddings, parts)
    else:
        sources = fetch_many(embeddings, need_ids, block_count)
        spread = spread_tiles(tile_rows, tile_cols, tile_count, tiles, sources, embeddings)
        size = spread.shape[0] // parts
        quarters = [lax.dynamic_slice_in_dim(spread, (me ^ k) * size, size, 0) for k in range(parts)]
    xs = [quarters[0]] + [exchange(quarters[k], "beh", k) for k in range(1, parts)]
    w_qkv = jnp.concatenate([w_query, w_key, w_value], axis=1).T
    merged = merge(xs, w_qkv, w_out, mlp_gain[None], w_up, w_down)
    back = [merged[0]] + [exchange(merged[k], "beh", k) for k in range(1, parts)]
    return place_parts(back)[None]


def solution(mesh):
    in_specs = (
        P("node", None),
        P("beh", "node", None, None),
        P("beh", "node"),
        P("beh", "node"),
        P("beh", "node"),
        P("beh", "node"),
        P(),
        P(),
        P(),
        P(),
        P(),
        P(),
        P(),
    )
    out_specs = P("beh", "node", None)
    return jax.shard_map(shards, mesh=mesh, in_specs=in_specs, out_specs=out_specs, check_vma=False)
```

```python
import functools
import math

import jax
import jax.numpy as jnp
from jax import lax
from jax.experimental import pallas as pl
from jax.experimental.pallas import tpu as pltpu
from jax.sharding import PartitionSpec as P

TB = 128
HEADS = 4
HEAD = 32
F32 = jnp.float32
BF16 = jnp.bfloat16
SMEM = pl.BlockSpec(memory_space=pltpu.SMEM)
VMEM = pl.BlockSpec(memory_space=pltpu.VMEM)
ANY = pl.BlockSpec(memory_space=pl.ANY)
HBM = pl.BlockSpec(memory_space=pltpu.HBM)
VMEM_LIMIT = 48 * 2**20


def hbm(*values):
    return [pltpu.with_memory_space_constraint(v, pltpu.HBM) for v in values]


def vmem(*values):
    return [pltpu.with_memory_space_constraint(v, pltpu.VMEM) for v in values]


def exchange(value, axis, mask):
    pairs = [(source, source ^ mask) for source in range(lax.axis_size(axis))]
    return lax.ppermute(value, axis, pairs)


def beh_masks(parts):
    first, *rest = range(parts - 1, 0, -1)
    return [(0, 0), (first, first)] + list(zip(rest[::-1], rest))


def exchange_beh(value, masks):
    peers = lax.axis_size("node")
    pairs = [
        (b * peers + n, (b ^ masks[n % 2]) * peers + n) for b in range(lax.axis_size("beh")) for n in range(peers)
    ]
    return lax.ppermute(value, ("beh", "node"), pairs)


def part_of(k, parts):
    even, odd = beh_masks(parts)[k]
    return lax.axis_index("beh") ^ jnp.where(lax.axis_index("node") % 2 == 0, even, odd)


def params(**more):
    return pltpu.CompilerParams(vmem_limit_bytes=VMEM_LIMIT, **more)


def cost(flops, moved):
    return pl.CostEstimate(flops=flops, bytes_accessed=moved, transcendentals=0)


def cells_kernel(chunk, pairs, cell_count, *refs):
    rows, cols, count, tiles, out, total, held, row_list, col_list, sems = refs
    steps = tiles.shape[0] // chunk
    here = lax.axis_index("node") // 2
    lists = [
        pltpu.make_async_copy(source, target, sems.at[steps + k])
        for k, (source, target) in enumerate(((rows, row_list), (cols, col_list)))
    ]
    loads = [
        pltpu.make_async_copy(tiles.at[pl.ds(s * chunk, chunk)], held.at[s], sems.at[s]) for s in range(steps)
    ]
    for copy in lists + loads:
        copy.start()
    total[...] = jnp.zeros_like(total)
    for copy in lists:
        copy.wait()
    for step, load in enumerate(loads):
        load.wait()
        for i in range(chunk):
            slot = step * chunk + i
            cell = row_list[0, slot] * pairs + (col_list[0, slot] ^ here)
            cell = jnp.where(slot < count[0, 0], cell, cell_count)
            total[cell] += held[step, i].astype(F32)
    out[...] = total[:cell_count].astype(BF16)


def sum_cells(rows, cols, count, tiles, pairs, block_count):
    slots = tiles.shape[0]
    chunk = math.gcd(slots, 16)
    cell_count = pairs * block_count
    return pl.pallas_call(
        functools.partial(cells_kernel, chunk, pairs, cell_count),
        in_specs=[HBM, HBM, SMEM, HBM],
        out_specs=VMEM,
        out_shape=jax.ShapeDtypeStruct((cell_count, TB, TB), BF16),
        scratch_shapes=[
            pltpu.VMEM((cell_count + 1, TB, TB), F32),
            pltpu.VMEM((slots // chunk, chunk, TB, TB), BF16),
            pltpu.SMEM(rows.shape, jnp.int32),
            pltpu.SMEM(cols.shape, jnp.int32),
            pltpu.SemaphoreType.DMA((slots // chunk + 2,)),
        ],
        compiler_params=params(),
        cost_estimate=cost(0, tiles.size * 2),
        name="cells",
    )(*hbm(rows, cols), count, *hbm(tiles))


def load_kernel(source, out, sem):
    copy = pltpu.make_async_copy(source, out, sem)
    copy.start()
    copy.wait()


def load(source):
    return pl.pallas_call(
        load_kernel,
        in_specs=[HBM],
        out_specs=VMEM,
        out_shape=jax.ShapeDtypeStruct(source.shape, source.dtype),
        scratch_shapes=[pltpu.SemaphoreType.DMA],
        compiler_params=params(),
        cost_estimate=cost(0, source.size * 2),
        name="load",
    )(*hbm(source))


def serve_kernel(block_count, pairs, *refs):
    asks, (own, other), outs = refs[:pairs], refs[pairs : pairs + 2], refs[pairs + 2 : 2 * pairs + 2]
    lists, sems = refs[2 * pairs + 2 : -1], refs[-1]
    here = lax.axis_index("node") // 2
    core = lax.axis_index("node") % 2
    copies = [
        pltpu.make_async_copy(ask, target, sems.at[k]) for k, (ask, target) in enumerate(zip(asks, lists))
    ]
    for copy in copies:
        copy.start()
    for copy in copies:
        copy.wait()
    for k, out in enumerate(outs):
        block = lists[k][0, here] - 2 * here * block_count
        upper = (block >= block_count).astype(jnp.int32)
        start = pl.multiple_of((block - upper * block_count) * TB, TB)

        @pl.when(upper == core)
        def _():
            out[...] = own[pl.ds(start, TB), :]

        @pl.when(upper != core)
        def _():
            out[...] = other[pl.ds(start, TB), :]


def serve(asks, own, other, block_count):
    pairs = len(asks)
    return pl.pallas_call(
        functools.partial(serve_kernel, block_count, pairs),
        in_specs=[ANY] * pairs + [VMEM] * 2,
        out_specs=[VMEM] * pairs,
        out_shape=[jax.ShapeDtypeStruct((TB, own.shape[1]), own.dtype)] * pairs,
        scratch_shapes=[pltpu.SMEM(asks[0].shape, jnp.int32)] * pairs + [pltpu.SemaphoreType.DMA((pairs,))],
        compiler_params=params(),
        name="serve",
    )(*asks, own, other)


def spread_kernel(pairs, cells, *refs):
    sources, own, outs = refs[:pairs], refs[pairs], refs[pairs + 1 :]
    stack = jnp.concatenate([s[...] for s in sources], axis=0)
    size = outs[0].shape[0]
    for k, out in enumerate(outs):
        part = part_of(k, len(outs))
        start = pl.multiple_of(part * size, size)
        block = part * (size // TB)
        for r in range(size // TB):
            lhs = jnp.concatenate([cells[(block + r) * pairs + m] for m in range(pairs)], axis=1)
            total = jnp.dot(lhs, stack, preferred_element_type=F32)
            rows = own[pl.ds(start + r * TB, TB), :].astype(F32)
            out[r * TB : (r + 1) * TB, :] = (total + rows).astype(BF16)


def spread_cells(cells, sources, own, parts):
    size = own.shape[0] // parts
    return pl.pallas_call(
        functools.partial(spread_kernel, len(sources)),
        in_specs=[VMEM] * (len(sources) + 2),
        out_specs=[VMEM] * parts,
        out_shape=[jax.ShapeDtypeStruct((size, own.shape[1]), BF16)] * parts,
        compiler_params=params(),
        name="spread",
    )(cells, *sources, own)


def project_kernel(w_qkv, x, out):
    feature = x.shape[1]
    full = lax.dot_general(w_qkv[...], x[...], (((1,), (1,)), ((), ())), preferred_element_type=F32)
    scale = math.log2(math.e) / math.sqrt(HEAD)
    out[:feature] = full[:feature] * scale
    out[feature:] = full[feature:]


def project(w_qkv, x):
    return pl.pallas_call(
        project_kernel,
        in_specs=[VMEM] * 2,
        out_specs=VMEM,
        out_shape=jax.ShapeDtypeStruct((w_qkv.shape[0], x.shape[0]), F32),
        compiler_params=params(),
        cost_estimate=cost(2 * w_qkv.size * x.shape[0], w_qkv.size),
        name="project",
    )(w_qkv, x)


def merge_kernel(count, which, tile, *refs):
    x = refs[0]
    projected = refs[1 : count + 1]
    w_out, gain, w_up, w_down, out = refs[count + 1 :]
    feature = w_out.shape[0]
    for step in range(x.shape[0] // tile):
        rows = pl.ds(step * tile, tile)
        query = projected[which][:feature, rows].reshape(HEADS, HEAD, tile)
        scores = [
            jnp.sum(query * p[feature : 2 * feature, rows].reshape(HEADS, HEAD, tile), axis=1, keepdims=True)
            for p in projected
        ]
        top = functools.reduce(jnp.maximum, scores)
        weights = [jnp.exp2(s - top) for s in scores]
        inverse = 1.0 / functools.reduce(jnp.add, weights)
        mixture = functools.reduce(
            jnp.add,
            [
                (w * inverse) * p[2 * feature :, rows].reshape(HEADS, HEAD, tile)
                for w, p in zip(weights, projected)
            ],
        )
        mixture = mixture.reshape(feature, tile).astype(BF16)
        residual = x[rows, :].astype(F32) + lax.dot_general(
            mixture, w_out[...], (((0,), (0,)), ((), ())), preferred_element_type=F32
        )
        meansq = jnp.mean(residual * residual, axis=-1, keepdims=True)
        normed = (residual * lax.rsqrt(meansq + 1e-06) * gain[...]).astype(BF16)
        half = 0.5 * jnp.dot(normed, w_up[...], preferred_element_type=F32)
        hidden = (half + half * jnp.tanh(half)).astype(BF16)
        result = residual + jnp.dot(hidden, w_down[...], preferred_element_type=F32)
        out[rows, :] = result.astype(BF16)


def merge(x, projected, which, w_out, gain, w_up, w_down):
    size, feature = x.shape
    tile = math.gcd(size, 512)
    return pl.pallas_call(
        functools.partial(merge_kernel, len(projected), which, tile),
        in_specs=[VMEM] * (len(projected) + 5),
        out_specs=VMEM,
        out_shape=jax.ShapeDtypeStruct((size, feature), BF16),
        compiler_params=params(),
        cost_estimate=cost(8 * size * w_up.size, w_up.size),
        name="merge",
    )(x, *projected, w_out, gain, w_up, w_down)


def place_kernel(*refs):
    parts, out, sems = refs[:-2], refs[-2], refs[-1]
    size = parts[0].shape[0]
    copies = []
    for k, part in enumerate(parts):
        start = pl.multiple_of(part_of(k, len(parts)) * size, size)
        copies.append(pltpu.make_async_copy(part, out.at[pl.ds(start, size), :], sems.at[k]))
        copies[-1].start()
    for copy in copies:
        copy.wait()


def place_parts(parts):
    size, feature = parts[0].shape
    return pl.pallas_call(
        place_kernel,
        in_specs=[VMEM] * len(parts),
        out_specs=HBM,
        out_shape=jax.ShapeDtypeStruct((size * len(parts), feature), BF16),
        scratch_shapes=[pltpu.SemaphoreType.DMA((len(parts),))],
        name="place",
    )(*vmem(*parts))


def tiles_kernel(chunk, rows, cols, count, tiles, sources, own, out, total):
    step = pl.program_id(0)

    @pl.when(step == 0)
    def _():
        total[...] = own[...].astype(F32)

    for i in range(chunk):
        slot = step * chunk + i

        @pl.when(slot < count[0, 0])
        def _():
            start = pl.multiple_of(rows[0, slot] * TB, TB)
            total[pl.ds(start, TB), :] += jnp.dot(
                tiles[i], sources[cols[0, slot]], preferred_element_type=F32
            )

    @pl.when(step == pl.num_programs(0) - 1)
    def _():
        out[...] = total[...].astype(BF16)


def spread_tiles(rows, cols, count, tiles, sources, own):
    slots = tiles.shape[0]
    chunk = math.gcd(slots, 16)
    return pl.pallas_call(
        functools.partial(tiles_kernel, chunk),
        grid=(slots // chunk,),
        in_specs=[SMEM] * 3
        + [
            pl.BlockSpec((chunk, TB, TB), lambda s: (s, 0, 0)),
            pl.BlockSpec(sources.shape, lambda s: (0, 0, 0)),
            pl.BlockSpec(own.shape, lambda s: (0, 0)),
        ],
        out_specs=pl.BlockSpec(own.shape, lambda s: (0, 0)),
        out_shape=jax.ShapeDtypeStruct(own.shape, BF16),
        scratch_shapes=[pltpu.VMEM(own.shape, F32)],
        compiler_params=params(),
        name="tiles",
    )(rows, cols, count, tiles, sources, own)


def fetch_many(embeddings, need_ids, block_count):
    peer_count = lax.axis_size("node")
    feature = embeddings.shape[1]
    needed = need_ids[0]
    owners = needed // block_count
    within = needed % block_count
    peer_ids = jnp.arange(peer_count, dtype=jnp.int32)
    matches = owners[:, None] == peer_ids[None, :]
    request = jnp.sum(jnp.where(matches, within[:, None] + 1, 0), axis=0)
    swapped = request.reshape(-1, 2)[:, ::-1].reshape(-1)
    request_pair = jnp.stack([request, swapped], axis=1)
    incoming = lax.all_to_all(request_pair, "node", split_axis=0, concat_axis=0, tiled=True)
    parity = lax.axis_index("node") % 2
    own = embeddings.reshape(block_count, TB, feature)
    other = exchange(embeddings, "node", 1).reshape(block_count, TB, feature)
    stack = jnp.concatenate([own, other], axis=0)
    codes = jnp.where(incoming[:, 0] > 0, incoming[:, 0], block_count + incoming[:, 1])
    half = TB // 2
    halves = lax.dynamic_slice_in_dim(stack, parity * half, half, 1)
    chooser = (codes[:, None] - 1 == jnp.arange(2 * block_count, dtype=jnp.int32)[None, :]).astype(BF16)
    outgoing = jnp.einsum("pk,kid->pid", chooser, halves, preferred_element_type=F32).astype(BF16)
    arrived = lax.all_to_all(outgoing, "node", split_axis=0, concat_axis=0, tiled=True)
    return arrived.reshape(peer_count // 2, TB, feature)


def shards(
    embeddings,
    adjacency,
    tile_rows,
    tile_cols,
    tile_count,
    need_ids,
    w_query,
    w_key,
    w_value,
    w_out,
    mlp_gain,
    w_up,
    w_down,
):
    parts = lax.axis_size("beh")
    pairs = lax.axis_size("node") // 2
    block_count = embeddings.shape[0] // TB
    tiles = adjacency[0]
    if pairs * block_count <= tiles.shape[0]:
        far = range(pairs - 1, 0, -1)
        asks = [exchange(need_ids, "node", 2 * k) for k in far] + hbm(need_ids)
        other = exchange(embeddings, "node", 1)
        own = load(embeddings)
        cells = sum_cells(tile_rows, tile_cols, tile_count, tiles, pairs, block_count)
        served = serve(asks[:1], own, other, block_count)
        *more, here = serve(asks[1:], own, other, block_count)
        sources = [here] + [exchange(block, "node", 2 * k) for k, block in zip(far, [*served, *more])][::-1]
        quarters = spread_cells(cells, sources, own, parts)
    else:
        sources = fetch_many(embeddings, need_ids, block_count)
        spread = spread_tiles(tile_rows, tile_cols, tile_count, tiles, sources, embeddings)
        size = spread.shape[0] // parts
        quarters = [lax.dynamic_slice_in_dim(spread, part_of(k, parts) * size, size, 0) for k in range(parts)]
    masks = beh_masks(parts)
    xs = [quarters[0]] + [exchange_beh(quarters[k], masks[k]) for k in range(1, parts)]
    w_qkv = jnp.concatenate([w_query, w_key, w_value], axis=1).T
    projected = [project(w_qkv, x) for x in xs]
    merged = [merge(xs[k], projected, k, w_out, mlp_gain[None], w_up, w_down) for k in range(parts)]
    back = [merged[0]] + [exchange_beh(merged[k], masks[k]) for k in range(1, parts)]
    return place_parts(back)[None]


def solution(mesh):
    in_specs = (
        P("node", None),
        P("beh", "node", None, None),
        P("beh", "node"),
        P("beh", "node"),
        P("beh", "node"),
        P("beh", "node"),
        P(),
        P(),
        P(),
        P(),
        P(),
        P(),
        P(),
    )
    out_specs = P("beh", "node", None)
    return jax.shard_map(shards, mesh=mesh, in_specs=in_specs, out_specs=out_specs, check_vma=False)
```

```python
import functools
import math

import jax
import jax.numpy as jnp
from jax import lax
from jax.experimental import pallas as pl
from jax.experimental.pallas import tpu as pltpu
from jax.sharding import PartitionSpec as P

TB = 128
HEADS = 4
HEAD = 32
F32 = jnp.float32
BF16 = jnp.bfloat16
SMEM = pl.BlockSpec(memory_space=pltpu.SMEM)
VMEM = pl.BlockSpec(memory_space=pltpu.VMEM)
ANY = pl.BlockSpec(memory_space=pl.ANY)
HBM = pl.BlockSpec(memory_space=pltpu.HBM)
VMEM_LIMIT = 48 * 2**20


def hbm(*values):
    return [pltpu.with_memory_space_constraint(v, pltpu.HBM) for v in values]


def vmem(*values):
    return [pltpu.with_memory_space_constraint(v, pltpu.VMEM) for v in values]


def exchange(value, axis, mask):
    pairs = [(source, source ^ mask) for source in range(lax.axis_size(axis))]
    return lax.ppermute(value, axis, pairs)


def beh_masks(parts):
    first, *rest = range(parts - 1, 0, -1)
    return [(0, 0)] + list(zip(rest, rest)) + [(first, first)]


def exchange_beh(value, masks):
    peers = lax.axis_size("node")
    pairs = [
        (b * peers + n, (b ^ masks[n % 2]) * peers + n) for b in range(lax.axis_size("beh")) for n in range(peers)
    ]
    return lax.ppermute(value, ("beh", "node"), pairs)


def part_of(k, parts):
    even, odd = beh_masks(parts)[k]
    return lax.axis_index("beh") ^ jnp.where(lax.axis_index("node") % 2 == 0, even, odd)


def params(**more):
    return pltpu.CompilerParams(vmem_limit_bytes=VMEM_LIMIT, **more)


def cost(flops, moved):
    return pl.CostEstimate(flops=flops, bytes_accessed=moved, transcendentals=0)


def cells_kernel(chunk, pairs, cell_count, *refs):
    rows, cols, count, tiles, out, total, held, row_list, col_list, sems = refs
    steps = tiles.shape[0] // chunk
    here = lax.axis_index("node") // 2
    lists = [
        pltpu.make_async_copy(source, target, sems.at[steps + k])
        for k, (source, target) in enumerate(((rows, row_list), (cols, col_list)))
    ]
    loads = [
        pltpu.make_async_copy(tiles.at[pl.ds(s * chunk, chunk)], held.at[s], sems.at[s]) for s in range(steps)
    ]
    for copy in lists + loads:
        copy.start()
    total[...] = jnp.zeros_like(total)
    for copy in lists:
        copy.wait()
    for step, load in enumerate(loads):
        load.wait()
        for i in range(chunk):
            slot = step * chunk + i
            cell = row_list[0, slot] * pairs + (col_list[0, slot] ^ here)
            cell = jnp.where(slot < count[0, 0], cell, cell_count)
            total[cell] += held[step, i].astype(F32)
    out[...] = total[:cell_count].astype(BF16)


def sum_cells(rows, cols, count, tiles, pairs, block_count):
    slots = tiles.shape[0]
    chunk = math.gcd(slots, 16)
    cell_count = pairs * block_count
    return pl.pallas_call(
        functools.partial(cells_kernel, chunk, pairs, cell_count),
        in_specs=[HBM, HBM, SMEM, HBM],
        out_specs=VMEM,
        out_shape=jax.ShapeDtypeStruct((cell_count, TB, TB), BF16),
        scratch_shapes=[
            pltpu.VMEM((cell_count + 1, TB, TB), F32),
            pltpu.VMEM((slots // chunk, chunk, TB, TB), BF16),
            pltpu.SMEM(rows.shape, jnp.int32),
            pltpu.SMEM(cols.shape, jnp.int32),
            pltpu.SemaphoreType.DMA((slots // chunk + 2,)),
        ],
        compiler_params=params(),
        cost_estimate=cost(0, tiles.size * 2),
        name="cells",
    )(*hbm(rows, cols), count, *hbm(tiles))


def load_kernel(source, out, sem):
    copy = pltpu.make_async_copy(source, out, sem)
    copy.start()
    copy.wait()


def load(source):
    return pl.pallas_call(
        load_kernel,
        in_specs=[HBM],
        out_specs=VMEM,
        out_shape=jax.ShapeDtypeStruct(source.shape, source.dtype),
        scratch_shapes=[pltpu.SemaphoreType.DMA],
        compiler_params=params(),
        cost_estimate=cost(0, source.size * 2),
        name="load",
    )(*hbm(source))


def serve_kernel(block_count, pairs, *refs):
    asks, (own, other), outs = refs[:pairs], refs[pairs : pairs + 2], refs[pairs + 2 : 2 * pairs + 2]
    lists, sems = refs[2 * pairs + 2 : -1], refs[-1]
    here = lax.axis_index("node") // 2
    core = lax.axis_index("node") % 2
    copies = [
        pltpu.make_async_copy(ask, target, sems.at[k]) for k, (ask, target) in enumerate(zip(asks, lists))
    ]
    for copy in copies:
        copy.start()
    for copy in copies:
        copy.wait()
    for k, out in enumerate(outs):
        block = lists[k][0, here] - 2 * here * block_count
        upper = (block >= block_count).astype(jnp.int32)
        start = pl.multiple_of((block - upper * block_count) * TB, TB)

        @pl.when(upper == core)
        def _():
            out[...] = own[pl.ds(start, TB), :]

        @pl.when(upper != core)
        def _():
            out[...] = other[pl.ds(start, TB), :]


def serve(asks, own, other, block_count):
    pairs = len(asks)
    return pl.pallas_call(
        functools.partial(serve_kernel, block_count, pairs),
        in_specs=[ANY] * pairs + [VMEM] * 2,
        out_specs=[VMEM] * pairs,
        out_shape=[jax.ShapeDtypeStruct((TB, own.shape[1]), own.dtype)] * pairs,
        scratch_shapes=[pltpu.SMEM(asks[0].shape, jnp.int32)] * pairs + [pltpu.SemaphoreType.DMA((pairs,))],
        compiler_params=params(),
        name="serve",
    )(*asks, own, other)


def spread_kernel(pairs, which, parts, cells, *refs):
    sources, own, outs = refs[:pairs], refs[pairs], refs[pairs + 1 :]
    stack = jnp.concatenate([s[...] for s in sources], axis=0)
    size = outs[0].shape[0]
    for k, out in zip(which, outs):
        part = part_of(k, parts)
        start = pl.multiple_of(part * size, size)
        block = part * (size // TB)
        for r in range(size // TB):
            lhs = jnp.concatenate([cells[(block + r) * pairs + m] for m in range(pairs)], axis=1)
            total = jnp.dot(lhs, stack, preferred_element_type=F32)
            rows = own[pl.ds(start + r * TB, TB), :].astype(F32)
            out[r * TB : (r + 1) * TB, :] = (total + rows).astype(BF16)


def spread_cells(cells, sources, own, which, parts):
    size = own.shape[0] // parts
    return pl.pallas_call(
        functools.partial(spread_kernel, len(sources), which, parts),
        in_specs=[VMEM] * (len(sources) + 2),
        out_specs=[VMEM] * len(which),
        out_shape=[jax.ShapeDtypeStruct((size, own.shape[1]), BF16)] * len(which),
        compiler_params=params(),
        name="spread",
    )(cells, *sources, own)


def project_kernel(w_qkv, x, *refs):
    out = refs[-1]
    feature = x.shape[1]
    full = lax.dot_general(w_qkv[...], x[...], (((1,), (1,)), ((), ())), preferred_element_type=F32)
    scale = math.log2(math.e) / math.sqrt(HEAD)
    out[:feature] = full[:feature] * scale
    out[feature:] = full[feature:]


def project(w_qkv, x, *before):
    return pl.pallas_call(
        project_kernel,
        in_specs=[VMEM] * (2 + len(before)),
        out_specs=VMEM,
        out_shape=jax.ShapeDtypeStruct((w_qkv.shape[0], x.shape[0]), F32),
        compiler_params=params(),
        cost_estimate=cost(2 * w_qkv.size * x.shape[0], w_qkv.size),
        name="project",
    )(w_qkv, x, *before)


def merge_kernel(count, which, tile, *refs):
    x = refs[0]
    projected = refs[1 : count + 1]
    w_out, gain, w_up, w_down, out = refs[count + 1 :]
    feature = w_out.shape[0]
    for step in range(x.shape[0] // tile):
        rows = pl.ds(step * tile, tile)
        query = projected[which][:feature, rows].reshape(HEADS, HEAD, tile)
        scores = [
            jnp.sum(query * p[feature : 2 * feature, rows].reshape(HEADS, HEAD, tile), axis=1, keepdims=True)
            for p in projected
        ]
        top = functools.reduce(jnp.maximum, scores)
        weights = [jnp.exp2(s - top) for s in scores]
        inverse = 1.0 / functools.reduce(jnp.add, weights)
        mixture = functools.reduce(
            jnp.add,
            [
                (w * inverse) * p[2 * feature :, rows].reshape(HEADS, HEAD, tile)
                for w, p in zip(weights, projected)
            ],
        )
        mixture = mixture.reshape(feature, tile).astype(BF16)
        residual = x[rows, :].astype(F32) + lax.dot_general(
            mixture, w_out[...], (((0,), (0,)), ((), ())), preferred_element_type=F32
        )
        meansq = jnp.mean(residual * residual, axis=-1, keepdims=True)
        normed = (residual * lax.rsqrt(meansq + 1e-06) * gain[...]).astype(BF16)
        half = 0.5 * jnp.dot(normed, w_up[...], preferred_element_type=F32)
        hidden = (half + half * jnp.tanh(half)).astype(BF16)
        result = residual + jnp.dot(hidden, w_down[...], preferred_element_type=F32)
        out[rows, :] = result.astype(BF16)


def merge(x, projected, which, w_out, gain, w_up, w_down):
    size, feature = x.shape
    tile = math.gcd(size, 512)
    return pl.pallas_call(
        functools.partial(merge_kernel, len(projected), which, tile),
        in_specs=[VMEM] * (len(projected) + 5),
        out_specs=VMEM,
        out_shape=jax.ShapeDtypeStruct((size, feature), BF16),
        compiler_params=params(),
        cost_estimate=cost(8 * size * w_up.size, w_up.size),
        name="merge",
    )(x, *projected, w_out, gain, w_up, w_down)


def place_kernel(which, parts, *refs):
    pieces, out, sems = refs[: len(which)], refs[-2], refs[-1]
    size = pieces[0].shape[0]
    copies = []
    for slot, (k, piece) in enumerate(zip(which, pieces)):
        start = pl.multiple_of(part_of(k, parts) * size, size)
        copies.append(pltpu.make_async_copy(piece, out.at[pl.ds(start, size), :], sems.at[slot]))
        copies[-1].start()
    for copy in copies:
        copy.wait()


def place_parts(pieces, which, parts, *begun):
    size, feature = pieces[0].shape
    return pl.pallas_call(
        functools.partial(place_kernel, which, parts),
        in_specs=[VMEM] * len(pieces) + [HBM] * len(begun),
        out_specs=HBM,
        out_shape=jax.ShapeDtypeStruct((size * parts, feature), BF16),
        scratch_shapes=[pltpu.SemaphoreType.DMA((len(pieces),))],
        input_output_aliases={len(pieces): 0} if begun else {},
        compiler_params=params(),
        name="place",
    )(*vmem(*pieces), *begun)


def tiles_kernel(chunk, rows, cols, count, tiles, sources, own, out, total):
    step = pl.program_id(0)

    @pl.when(step == 0)
    def _():
        total[...] = own[...].astype(F32)

    for i in range(chunk):
        slot = step * chunk + i

        @pl.when(slot < count[0, 0])
        def _():
            start = pl.multiple_of(rows[0, slot] * TB, TB)
            total[pl.ds(start, TB), :] += jnp.dot(
                tiles[i], sources[cols[0, slot]], preferred_element_type=F32
            )

    @pl.when(step == pl.num_programs(0) - 1)
    def _():
        out[...] = total[...].astype(BF16)


def spread_tiles(rows, cols, count, tiles, sources, own):
    slots = tiles.shape[0]
    chunk = math.gcd(slots, 16)
    return pl.pallas_call(
        functools.partial(tiles_kernel, chunk),
        grid=(slots // chunk,),
        in_specs=[SMEM] * 3
        + [
            pl.BlockSpec((chunk, TB, TB), lambda s: (s, 0, 0)),
            pl.BlockSpec(sources.shape, lambda s: (0, 0, 0)),
            pl.BlockSpec(own.shape, lambda s: (0, 0)),
        ],
        out_specs=pl.BlockSpec(own.shape, lambda s: (0, 0)),
        out_shape=jax.ShapeDtypeStruct(own.shape, BF16),
        scratch_shapes=[pltpu.VMEM(own.shape, F32)],
        compiler_params=params(),
        name="tiles",
    )(rows, cols, count, tiles, sources, own)


def fetch_many(embeddings, need_ids, block_count):
    peer_count = lax.axis_size("node")
    feature = embeddings.shape[1]
    needed = need_ids[0]
    owners = needed // block_count
    within = needed % block_count
    peer_ids = jnp.arange(peer_count, dtype=jnp.int32)
    matches = owners[:, None] == peer_ids[None, :]
    request = jnp.sum(jnp.where(matches, within[:, None] + 1, 0), axis=0)
    swapped = request.reshape(-1, 2)[:, ::-1].reshape(-1)
    request_pair = jnp.stack([request, swapped], axis=1)
    incoming = lax.all_to_all(request_pair, "node", split_axis=0, concat_axis=0, tiled=True)
    parity = lax.axis_index("node") % 2
    own = embeddings.reshape(block_count, TB, feature)
    other = exchange(embeddings, "node", 1).reshape(block_count, TB, feature)
    stack = jnp.concatenate([own, other], axis=0)
    codes = jnp.where(incoming[:, 0] > 0, incoming[:, 0], block_count + incoming[:, 1])
    half = TB // 2
    halves = lax.dynamic_slice_in_dim(stack, parity * half, half, 1)
    chooser = (codes[:, None] - 1 == jnp.arange(2 * block_count, dtype=jnp.int32)[None, :]).astype(BF16)
    outgoing = jnp.einsum("pk,kid->pid", chooser, halves, preferred_element_type=F32).astype(BF16)
    arrived = lax.all_to_all(outgoing, "node", split_axis=0, concat_axis=0, tiled=True)
    return arrived.reshape(peer_count // 2, TB, feature)


def shards(
    embeddings,
    adjacency,
    tile_rows,
    tile_cols,
    tile_count,
    need_ids,
    w_query,
    w_key,
    w_value,
    w_out,
    mlp_gain,
    w_up,
    w_down,
):
    parts = lax.axis_size("beh")
    pairs = lax.axis_size("node") // 2
    block_count = embeddings.shape[0] // TB
    tiles = adjacency[0]
    if pairs * block_count <= tiles.shape[0]:
        far = range(pairs - 1, 0, -1)
        asks = [exchange(need_ids, "node", 2 * k) for k in far] + hbm(need_ids)
        other = exchange(embeddings, "node", 1)
        own = load(embeddings)
        cells = sum_cells(tile_rows, tile_cols, tile_count, tiles, pairs, block_count)
        served = serve(asks[:1], own, other, block_count)
        *more, here = serve(asks[1:], own, other, block_count)
        sources = [here] + [exchange(block, "node", 2 * k) for k, block in zip(far, [*served, *more])][::-1]
        last = spread_cells(cells, sources, own, [parts - 1], parts)
        quarters = spread_cells(cells, sources, own, list(range(parts - 1)), parts) + last
    else:
        sources = fetch_many(embeddings, need_ids, block_count)
        spread = spread_tiles(tile_rows, tile_cols, tile_count, tiles, sources, embeddings)
        size = spread.shape[0] // parts
        quarters = [lax.dynamic_slice_in_dim(spread, part_of(k, parts) * size, size, 0) for k in range(parts)]
    masks = beh_masks(parts)
    xs = [quarters[0]] + [exchange_beh(quarters[k], masks[k]) for k in range(1, parts)]
    w_qkv = jnp.concatenate([w_query, w_key, w_value], axis=1).T
    order = [parts - 1, *range(1, parts - 1), 0]
    projected = [project(w_qkv, xs[0])] * parts
    for k, before in zip(order[:-1], order[-1:] + order):
        projected[k] = project(w_qkv, xs[k], projected[before])
    merged = [merge(xs[k], projected, k, w_out, mlp_gain[None], w_up, w_down) for k in order]
    back = [exchange_beh(part, masks[k]) if k else part for k, part in zip(order, merged)]
    late = parts - 2
    begun = place_parts(back[:late] + back[late + 1 :], order[:late] + order[late + 1 :], parts)
    return place_parts(back[late : late + 1], order[late : late + 1], parts, begun)[None]


def solution(mesh):
    in_specs = (
        P("node", None),
        P("beh", "node", None, None),
        P("beh", "node"),
        P("beh", "node"),
        P("beh", "node"),
        P("beh", "node"),
        P(),
        P(),
        P(),
        P(),
        P(),
        P(),
        P(),
    )
    out_specs = P("beh", "node", None)
    return jax.shard_map(shards, mesh=mesh, in_specs=in_specs, out_specs=out_specs, check_vma=False)
```

```python
import functools
import math

import jax
import jax.numpy as jnp
from jax import lax
from jax.experimental import pallas as pl
from jax.experimental.pallas import tpu as pltpu
from jax.sharding import PartitionSpec as P

TB = 128
HEADS = 4
HEAD = 32
F32 = jnp.float32
BF16 = jnp.bfloat16
SMEM = pl.BlockSpec(memory_space=pltpu.SMEM)
VMEM = pl.BlockSpec(memory_space=pltpu.VMEM)
ANY = pl.BlockSpec(memory_space=pl.ANY)
HBM = pl.BlockSpec(memory_space=pltpu.HBM)
VMEM_LIMIT = 48 * 2**20


def hbm(*values):
    return [pltpu.with_memory_space_constraint(v, pltpu.HBM) for v in values]


def vmem(*values):
    return [pltpu.with_memory_space_constraint(v, pltpu.VMEM) for v in values]


def exchange(value, axis, mask):
    pairs = [(source, source ^ mask) for source in range(lax.axis_size(axis))]
    return lax.ppermute(value, axis, pairs)


def beh_masks(parts):
    first, *rest = range(parts - 1, 0, -1)
    return [(0, 0)] + list(zip(rest, rest)) + [(first, first)]


def exchange_beh(value, masks):
    peers = lax.axis_size("node")
    pairs = [
        (b * peers + n, (b ^ masks[n % 2]) * peers + n) for b in range(lax.axis_size("beh")) for n in range(peers)
    ]
    return lax.ppermute(value, ("beh", "node"), pairs)


def part_of(k, parts):
    even, odd = beh_masks(parts)[k]
    return lax.axis_index("beh") ^ jnp.where(lax.axis_index("node") % 2 == 0, even, odd)


def params(**more):
    return pltpu.CompilerParams(vmem_limit_bytes=VMEM_LIMIT, **more)


def cost(flops, moved):
    return pl.CostEstimate(flops=flops, bytes_accessed=moved, transcendentals=0)


def cells_kernel(chunk, pairs, cell_count, *refs):
    rows, cols, count, tiles, out, total, held, row_list, col_list, sems = refs
    steps = tiles.shape[0] // chunk
    here = lax.axis_index("node") // 2
    lists = [
        pltpu.make_async_copy(source, target, sems.at[steps + k])
        for k, (source, target) in enumerate(((rows, row_list), (cols, col_list)))
    ]
    loads = [
        pltpu.make_async_copy(tiles.at[pl.ds(s * chunk, chunk)], held.at[s], sems.at[s]) for s in range(steps)
    ]
    for copy in lists + loads:
        copy.start()
    total[...] = jnp.zeros_like(total)
    for copy in lists:
        copy.wait()
    for step, load in enumerate(loads):
        load.wait()
        for i in range(chunk):
            slot = step * chunk + i
            cell = row_list[0, slot] * pairs + (col_list[0, slot] ^ here)
            cell = jnp.where(slot < count[0, 0], cell, cell_count)
            total[cell] += held[step, i].astype(F32)
    out[...] = total[:cell_count].astype(BF16)


def sum_cells(rows, cols, count, tiles, pairs, block_count):
    slots = tiles.shape[0]
    chunk = math.gcd(slots, 16)
    cell_count = pairs * block_count
    return pl.pallas_call(
        functools.partial(cells_kernel, chunk, pairs, cell_count),
        in_specs=[HBM, HBM, SMEM, HBM],
        out_specs=VMEM,
        out_shape=jax.ShapeDtypeStruct((cell_count, TB, TB), BF16),
        scratch_shapes=[
            pltpu.VMEM((cell_count + 1, TB, TB), F32),
            pltpu.VMEM((slots // chunk, chunk, TB, TB), BF16),
            pltpu.SMEM(rows.shape, jnp.int32),
            pltpu.SMEM(cols.shape, jnp.int32),
            pltpu.SemaphoreType.DMA((slots // chunk + 2,)),
        ],
        compiler_params=params(),
        cost_estimate=cost(0, tiles.size * 2),
        name="cells",
    )(*hbm(rows, cols), count, *hbm(tiles))


def load_kernel(*refs):
    half = len(refs) // 2
    sems = refs[-1]
    copies = [pltpu.make_async_copy(refs[k], refs[half + k], sems.at[k]) for k in range(half)]
    for copy in copies:
        copy.start()
    for copy in copies:
        copy.wait()


def load(*sources):
    return pl.pallas_call(
        load_kernel,
        in_specs=[HBM] * len(sources),
        out_specs=[VMEM] * len(sources),
        out_shape=[jax.ShapeDtypeStruct(s.shape, s.dtype) for s in sources],
        scratch_shapes=[pltpu.SemaphoreType.DMA((len(sources),))],
        compiler_params=params(),
        cost_estimate=cost(0, sum(s.size * 2 for s in sources)),
        name="load",
    )(*hbm(*sources))


def serve_kernel(block_count, pairs, *refs):
    asks, (own, other), outs = refs[:pairs], refs[pairs : pairs + 2], refs[pairs + 2 : 2 * pairs + 2]
    lists, sems = refs[2 * pairs + 2 : -1], refs[-1]
    here = lax.axis_index("node") // 2
    core = lax.axis_index("node") % 2
    copies = [
        pltpu.make_async_copy(ask, target, sems.at[k]) for k, (ask, target) in enumerate(zip(asks, lists))
    ]
    for copy in copies:
        copy.start()
    for copy in copies:
        copy.wait()
    for k, out in enumerate(outs):
        block = lists[k][0, here] - 2 * here * block_count
        upper = (block >= block_count).astype(jnp.int32)
        start = pl.multiple_of((block - upper * block_count) * TB, TB)

        @pl.when(upper == core)
        def _():
            out[...] = own[pl.ds(start, TB), :]

        @pl.when(upper != core)
        def _():
            out[...] = other[pl.ds(start, TB), :]


def serve(asks, own, other, block_count, weight):
    pairs = len(asks)
    return pl.pallas_call(
        functools.partial(serve_kernel, block_count, pairs),
        in_specs=[ANY] * pairs + [VMEM] * 2,
        out_specs=[VMEM] * pairs,
        out_shape=[jax.ShapeDtypeStruct((TB, own.shape[1]), own.dtype)] * pairs,
        scratch_shapes=[pltpu.SMEM(asks[0].shape, jnp.int32)] * pairs + [pltpu.SemaphoreType.DMA((pairs,))],
        compiler_params=params(),
        cost_estimate=cost(weight, own.size),
        name="serve",
    )(*asks, own, other)


def begin_kernel(pairs, columns, cells, *refs):
    sources, own, out = refs[: len(columns)], refs[-2], refs[-1]
    stack = jnp.concatenate([s[...] for s in sources], axis=0)
    for r in range(own.shape[0] // TB):
        rows = pl.ds(r * TB, TB)
        lhs = jnp.concatenate([cells[r * pairs + m] for m in columns], axis=1)
        out[rows, :] = own[rows, :].astype(F32) + jnp.dot(lhs, stack, preferred_element_type=F32)


def begin_spread(cells, sources, columns, own, pairs):
    return pl.pallas_call(
        functools.partial(begin_kernel, pairs, columns),
        in_specs=[VMEM] * (len(sources) + 2),
        out_specs=VMEM,
        out_shape=jax.ShapeDtypeStruct(own.shape, F32),
        compiler_params=params(),
        cost_estimate=cost(2 * own.size * TB * len(columns), own.size * 2),
        name="begin",
    )(cells, *sources, own)


def spread_kernel(pairs, columns, which, parts, cells, *refs):
    sources, begun, outs = refs[: len(columns)], refs[len(columns)], refs[len(columns) + 1 :]
    stack = jnp.concatenate([s[...] for s in sources], axis=0)
    size = outs[0].shape[0]
    for k, out in zip(which, outs):
        part = part_of(k, parts)
        start = pl.multiple_of(part * size, size)
        block = part * (size // TB)
        for r in range(size // TB):
            lhs = jnp.concatenate([cells[(block + r) * pairs + m] for m in columns], axis=1)
            total = jnp.dot(lhs, stack, preferred_element_type=F32)
            out[r * TB : (r + 1) * TB, :] = (begun[pl.ds(start + r * TB, TB), :] + total).astype(BF16)


def spread_cells(cells, sources, columns, begun, which, parts, pairs):
    size = begun.shape[0] // parts
    return pl.pallas_call(
        functools.partial(spread_kernel, pairs, columns, which, parts),
        in_specs=[VMEM] * (len(sources) + 2),
        out_specs=[VMEM] * len(which),
        out_shape=[jax.ShapeDtypeStruct((size, begun.shape[1]), BF16)] * len(which),
        compiler_params=params(),
        name="spread",
    )(cells, *sources, begun)


def project_kernel(w_qkv, x, *refs):
    out = refs[-1]
    feature = x.shape[1]
    full = lax.dot_general(w_qkv[...], x[...], (((1,), (1,)), ((), ())), preferred_element_type=F32)
    scale = math.log2(math.e) / math.sqrt(HEAD)
    out[:feature] = full[:feature] * scale
    out[feature:] = full[feature:]


def project(w_qkv, x, *before):
    return pl.pallas_call(
        project_kernel,
        in_specs=[VMEM] * (2 + len(before)),
        out_specs=VMEM,
        out_shape=jax.ShapeDtypeStruct((w_qkv.shape[0], x.shape[0]), F32),
        compiler_params=params(),
        cost_estimate=cost(2 * w_qkv.size * x.shape[0], w_qkv.size),
        name="project",
    )(w_qkv, x, *before)


def merge_kernel(count, which, tile, *refs):
    x = refs[0]
    projected = refs[1 : count + 1]
    w_out, gain, w_up, w_down, out = refs[count + 1 :]
    feature = w_out.shape[0]
    for step in range(x.shape[0] // tile):
        rows = pl.ds(step * tile, tile)
        query = projected[which][:feature, rows].reshape(HEADS, HEAD, tile)
        scores = [
            jnp.sum(query * p[feature : 2 * feature, rows].reshape(HEADS, HEAD, tile), axis=1, keepdims=True)
            for p in projected
        ]
        top = functools.reduce(jnp.maximum, scores)
        weights = [jnp.exp2(s - top) for s in scores]
        inverse = 1.0 / functools.reduce(jnp.add, weights)
        mixture = functools.reduce(
            jnp.add,
            [
                (w * inverse) * p[2 * feature :, rows].reshape(HEADS, HEAD, tile)
                for w, p in zip(weights, projected)
            ],
        )
        mixture = mixture.reshape(feature, tile).astype(BF16)
        residual = x[rows, :].astype(F32) + lax.dot_general(
            mixture, w_out[...], (((0,), (0,)), ((), ())), preferred_element_type=F32
        )
        meansq = jnp.mean(residual * residual, axis=-1, keepdims=True)
        normed = (residual * lax.rsqrt(meansq + 1e-06) * gain[...]).astype(BF16)
        half = 0.5 * jnp.dot(normed, w_up[...], preferred_element_type=F32)
        hidden = (half + half * jnp.tanh(half)).astype(BF16)
        result = residual + jnp.dot(hidden, w_down[...], preferred_element_type=F32)
        out[rows, :] = result.astype(BF16)


def merge(x, projected, which, w_out, gain, w_up, w_down):
    size, feature = x.shape
    tile = math.gcd(size, 512)
    return pl.pallas_call(
        functools.partial(merge_kernel, len(projected), which, tile),
        in_specs=[VMEM] * (len(projected) + 5),
        out_specs=VMEM,
        out_shape=jax.ShapeDtypeStruct((size, feature), BF16),
        compiler_params=params(),
        cost_estimate=cost(8 * size * w_up.size, w_up.size),
        name="merge",
    )(x, *projected, w_out, gain, w_up, w_down)


def place_kernel(which, parts, *refs):
    pieces, out, sems = refs[: len(which)], refs[-2], refs[-1]
    size = pieces[0].shape[0]
    copies = []
    for slot, (k, piece) in enumerate(zip(which, pieces)):
        start = pl.multiple_of(part_of(k, parts) * size, size)
        copies.append(pltpu.make_async_copy(piece, out.at[pl.ds(start, size), :], sems.at[slot]))
        copies[-1].start()
    for copy in copies:
        copy.wait()


def place_parts(pieces, which, parts, *begun):
    size, feature = pieces[0].shape
    return pl.pallas_call(
        functools.partial(place_kernel, which, parts),
        in_specs=[VMEM] * len(pieces) + [HBM] * len(begun),
        out_specs=HBM,
        out_shape=jax.ShapeDtypeStruct((size * parts, feature), BF16),
        scratch_shapes=[pltpu.SemaphoreType.DMA((len(pieces),))],
        input_output_aliases={len(pieces): 0} if begun else {},
        compiler_params=params(),
        name="place",
    )(*vmem(*pieces), *begun)


def tiles_kernel(chunk, rows, cols, count, tiles, sources, own, out, total):
    step = pl.program_id(0)

    @pl.when(step == 0)
    def _():
        total[...] = own[...].astype(F32)

    for i in range(chunk):
        slot = step * chunk + i

        @pl.when(slot < count[0, 0])
        def _():
            start = pl.multiple_of(rows[0, slot] * TB, TB)
            total[pl.ds(start, TB), :] += jnp.dot(
                tiles[i], sources[cols[0, slot]], preferred_element_type=F32
            )

    @pl.when(step == pl.num_programs(0) - 1)
    def _():
        out[...] = total[...].astype(BF16)


def spread_tiles(rows, cols, count, tiles, sources, own):
    slots = tiles.shape[0]
    chunk = math.gcd(slots, 16)
    return pl.pallas_call(
        functools.partial(tiles_kernel, chunk),
        grid=(slots // chunk,),
        in_specs=[SMEM] * 3
        + [
            pl.BlockSpec((chunk, TB, TB), lambda s: (s, 0, 0)),
            pl.BlockSpec(sources.shape, lambda s: (0, 0, 0)),
            pl.BlockSpec(own.shape, lambda s: (0, 0)),
        ],
        out_specs=pl.BlockSpec(own.shape, lambda s: (0, 0)),
        out_shape=jax.ShapeDtypeStruct(own.shape, BF16),
        scratch_shapes=[pltpu.VMEM(own.shape, F32)],
        compiler_params=params(),
        name="tiles",
    )(rows, cols, count, tiles, sources, own)


def fetch_many(embeddings, need_ids, block_count):
    peer_count = lax.axis_size("node")
    feature = embeddings.shape[1]
    needed = need_ids[0]
    owners = needed // block_count
    within = needed % block_count
    peer_ids = jnp.arange(peer_count, dtype=jnp.int32)
    matches = owners[:, None] == peer_ids[None, :]
    request = jnp.sum(jnp.where(matches, within[:, None] + 1, 0), axis=0)
    swapped = request.reshape(-1, 2)[:, ::-1].reshape(-1)
    request_pair = jnp.stack([request, swapped], axis=1)
    incoming = lax.all_to_all(request_pair, "node", split_axis=0, concat_axis=0, tiled=True)
    parity = lax.axis_index("node") % 2
    own = embeddings.reshape(block_count, TB, feature)
    other = exchange(embeddings, "node", 1).reshape(block_count, TB, feature)
    stack = jnp.concatenate([own, other], axis=0)
    codes = jnp.where(incoming[:, 0] > 0, incoming[:, 0], block_count + incoming[:, 1])
    half = TB // 2
    halves = lax.dynamic_slice_in_dim(stack, parity * half, half, 1)
    chooser = (codes[:, None] - 1 == jnp.arange(2 * block_count, dtype=jnp.int32)[None, :]).astype(BF16)
    outgoing = jnp.einsum("pk,kid->pid", chooser, halves, preferred_element_type=F32).astype(BF16)
    arrived = lax.all_to_all(outgoing, "node", split_axis=0, concat_axis=0, tiled=True)
    return arrived.reshape(peer_count // 2, TB, feature)


def shards(
    embeddings,
    adjacency,
    tile_rows,
    tile_cols,
    tile_count,
    need_ids,
    w_query,
    w_key,
    w_value,
    w_out,
    mlp_gain,
    w_up,
    w_down,
):
    parts = lax.axis_size("beh")
    pairs = lax.axis_size("node") // 2
    block_count = embeddings.shape[0] // TB
    tiles = adjacency[0]
    if pairs * block_count <= tiles.shape[0]:
        far = range(pairs - 1, 0, -1)
        own, ids = load(embeddings, need_ids)
        asks = [exchange(need_ids if k == pairs - 1 else ids, "node", 2 * k) for k in far] + [ids]
        other = exchange(embeddings, "node", 1)
        cells = sum_cells(tile_rows, tile_cols, tile_count, tiles, pairs, block_count)
        served = serve(asks[:1], own, other, block_count, 10**10)
        *more, here = serve(asks[1:], own, other, block_count, 10**10)
        first, *rest = [exchange(block, "node", 2 * k) for k, block in zip(far, [*served, *more])]
        begun = begin_spread(cells, [first, here], [pairs - 1, 0], own, pairs)
        arms = (cells, rest, list(far)[1:], begun)
        last = spread_cells(*arms, [parts - 1], parts, pairs)
        quarters = spread_cells(*arms, list(range(parts - 1)), parts, pairs) + last
    else:
        sources = fetch_many(embeddings, need_ids, block_count)
        spread = spread_tiles(tile_rows, tile_cols, tile_count, tiles, sources, embeddings)
        size = spread.shape[0] // parts
        quarters = [lax.dynamic_slice_in_dim(spread, part_of(k, parts) * size, size, 0) for k in range(parts)]
    masks = beh_masks(parts)
    xs = [quarters[0]] + [exchange_beh(quarters[k], masks[k]) for k in range(1, parts)]
    w_qkv = jnp.concatenate([w_query, w_key, w_value], axis=1).T
    order = [parts - 1, *range(1, parts - 1), 0]
    projected = [project(w_qkv, xs[0])] * parts
    for k, before in zip(order[:-1], order[-1:] + order):
        projected[k] = project(w_qkv, xs[k], projected[before])
    merged = [merge(xs[k], projected, k, w_out, mlp_gain[None], w_up, w_down) for k in order]
    back = [exchange_beh(part, masks[k]) if k else part for k, part in zip(order, merged)]
    late = parts - 2
    begun = place_parts(back[:late] + back[late + 1 :], order[:late] + order[late + 1 :], parts)
    return place_parts(back[late : late + 1], order[late : late + 1], parts, begun)[None]


def solution(mesh):
    in_specs = (
        P("node", None),
        P("beh", "node", None, None),
        P("beh", "node"),
        P("beh", "node"),
        P("beh", "node"),
        P("beh", "node"),
        P(),
        P(),
        P(),
        P(),
        P(),
        P(),
        P(),
    )
    out_specs = P("beh", "node", None)
    return jax.shard_map(shards, mesh=mesh, in_specs=in_specs, out_specs=out_specs, check_vma=False)
```

```python
import functools
import math

import jax
import jax.numpy as jnp
from jax import lax
from jax.experimental import pallas as pl
from jax.experimental.pallas import tpu as pltpu
from jax.sharding import PartitionSpec as P

TB = 128
HEADS = 4
HEAD = 32
F32 = jnp.float32
BF16 = jnp.bfloat16
SMEM = pl.BlockSpec(memory_space=pltpu.SMEM)
VMEM = pl.BlockSpec(memory_space=pltpu.VMEM)
ANY = pl.BlockSpec(memory_space=pl.ANY)
HBM = pl.BlockSpec(memory_space=pltpu.HBM)
VMEM_LIMIT = 48 * 2**20


def hbm(*values):
    return [pltpu.with_memory_space_constraint(v, pltpu.HBM) for v in values]


def vmem(*values):
    return [pltpu.with_memory_space_constraint(v, pltpu.VMEM) for v in values]


def exchange(value, axis, mask):
    pairs = [(source, source ^ mask) for source in range(lax.axis_size(axis))]
    return lax.ppermute(value, axis, pairs)


def beh_masks(parts):
    first, *rest = range(parts - 1, 0, -1)
    return [(0, 0)] + list(zip(rest, rest)) + [(first, first)]


def exchange_beh(value, masks):
    peers = lax.axis_size("node")
    pairs = [
        (b * peers + n, (b ^ masks[n % 2]) * peers + n) for b in range(lax.axis_size("beh")) for n in range(peers)
    ]
    return lax.ppermute(value, ("beh", "node"), pairs)


def part_of(k, parts):
    even, odd = beh_masks(parts)[k]
    return lax.axis_index("beh") ^ jnp.where(lax.axis_index("node") % 2 == 0, even, odd)


def params(**more):
    return pltpu.CompilerParams(vmem_limit_bytes=VMEM_LIMIT, **more)


def cost(flops, moved):
    return pl.CostEstimate(flops=flops, bytes_accessed=moved, transcendentals=0)


def cells_kernel(chunk, pairs, columns, rows, cols, count, tiles, *refs):
    sources, refs = refs[: len(columns)], refs[len(columns) :]
    own, out, begun, total, held, row_list, col_list, sems = refs
    steps = tiles.shape[0] // chunk
    block_count = own.shape[0] // TB
    here = lax.axis_index("node") // 2
    lists = [
        pltpu.make_async_copy(source, target, sems.at[steps + k])
        for k, (source, target) in enumerate(((rows, row_list), (cols, col_list)))
    ]
    loads = [
        pltpu.make_async_copy(tiles.at[pl.ds(s * chunk, chunk)], held.at[s], sems.at[s]) for s in range(steps)
    ]
    for copy in lists:
        copy.start()
    for step, load in enumerate(loads):
        pl.when(step * chunk < count[0, 0])(load.start)
    total[...] = jnp.zeros_like(total)
    for copy in lists:
        copy.wait()
    for step, load in enumerate(loads):

        @pl.when(step * chunk < count[0, 0])
        def _():
            load.wait()
            for i in range(chunk):
                slot = step * chunk + i
                cell = row_list[0, slot] * pairs + (col_list[0, slot] ^ here)
                cell = jnp.where(slot < count[0, 0], cell, block_count * pairs)
                total[cell] += held[step, i].astype(F32)

    stack = jnp.concatenate([s[...] for s in sources], axis=0)
    others = [m for m in range(pairs) if m not in columns]
    for r in range(block_count):
        rows_of = pl.ds(r * TB, TB)
        lhs = jnp.concatenate([total[r * pairs + m].astype(BF16) for m in columns], axis=1)
        begun[rows_of, :] = own[rows_of, :].astype(F32) + jnp.dot(lhs, stack, preferred_element_type=F32)
        for k, m in enumerate(others):
            out[r * len(others) + k] = total[r * pairs + m].astype(BF16)


def begin_spread(rows, cols, count, tiles, sources, columns, own, pairs):
    slots = tiles.shape[0]
    chunk = math.gcd(slots, 16)
    block_count = own.shape[0] // TB
    return pl.pallas_call(
        functools.partial(cells_kernel, chunk, pairs, columns),
        in_specs=[HBM, HBM, SMEM, HBM] + [VMEM] * (len(sources) + 1),
        out_specs=[VMEM] * 2,
        out_shape=[
            jax.ShapeDtypeStruct((block_count * (pairs - len(columns)), TB, TB), BF16),
            jax.ShapeDtypeStruct(own.shape, F32),
        ],
        scratch_shapes=[
            pltpu.VMEM((block_count * pairs + 1, TB, TB), F32),
            pltpu.VMEM((slots // chunk, chunk, TB, TB), BF16),
            pltpu.SMEM(rows.shape, jnp.int32),
            pltpu.SMEM(cols.shape, jnp.int32),
            pltpu.SemaphoreType.DMA((slots // chunk + 2,)),
        ],
        compiler_params=params(),
        cost_estimate=cost(0, tiles.size * 2),
        name="cells",
    )(*hbm(rows, cols), count, *hbm(tiles), *sources, own)


def load_kernel(*refs):
    half = len(refs) // 2
    sems = refs[-1]
    copies = [pltpu.make_async_copy(refs[k], refs[half + k], sems.at[k]) for k in range(half)]
    for copy in copies:
        copy.start()
    for copy in copies:
        copy.wait()


def load(*sources):
    return pl.pallas_call(
        load_kernel,
        in_specs=[HBM] * len(sources),
        out_specs=[VMEM] * len(sources),
        out_shape=[jax.ShapeDtypeStruct(s.shape, s.dtype) for s in sources],
        scratch_shapes=[pltpu.SemaphoreType.DMA((len(sources),))],
        compiler_params=params(),
        cost_estimate=cost(0, sum(s.size * 2 for s in sources)),
        name="load",
    )(*hbm(*sources))


def serve_kernel(block_count, pairs, *refs):
    asks, (own, other), outs = refs[:pairs], refs[pairs : pairs + 2], refs[pairs + 2 :]
    here = lax.axis_index("node") // 2
    core = lax.axis_index("node") % 2
    blocks = []
    for ask in asks:
        lanes = lax.broadcasted_iota(jnp.int32, ask.shape, 1)
        blocks.append(jnp.sum(jnp.where(lanes == here, ask[...], 0)) - 2 * here * block_count)
    for block, out in zip(blocks, outs):
        upper = (block >= block_count).astype(jnp.int32)
        start = pl.multiple_of((block - upper * block_count) * TB, TB)

        @pl.when(upper == core)
        def _():
            out[...] = own[pl.ds(start, TB), :]

        @pl.when(upper != core)
        def _():
            out[...] = other[pl.ds(start, TB), :]


def serve(asks, own, other, block_count, weight):
    pairs = len(asks)
    return pl.pallas_call(
        functools.partial(serve_kernel, block_count, pairs),
        in_specs=[VMEM] * (pairs + 2),
        out_specs=[VMEM] * pairs,
        out_shape=[jax.ShapeDtypeStruct((TB, own.shape[1]), own.dtype)] * pairs,
        compiler_params=params(),
        cost_estimate=cost(weight, own.size),
        name="serve",
    )(*asks, own, other)


def spread_kernel(columns, which, parts, cells, *refs):
    sources, begun, outs = refs[:columns], refs[columns], refs[columns + 1 :]
    stack = jnp.concatenate([s[...] for s in sources[::-1]], axis=0)
    size = outs[0].shape[0]
    for k, out in zip(which, outs):
        part = part_of(k, parts)
        start = pl.multiple_of(part * size, size)
        block = part * (size // TB)
        for r in range(size // TB):
            lhs = jnp.concatenate([cells[(block + r) * columns + m] for m in range(columns)], axis=1)
            total = jnp.dot(lhs, stack, preferred_element_type=F32)
            out[r * TB : (r + 1) * TB, :] = (begun[pl.ds(start + r * TB, TB), :] + total).astype(BF16)


def spread_cells(cells, sources, begun, which, parts):
    size = begun.shape[0] // parts
    return pl.pallas_call(
        functools.partial(spread_kernel, len(sources), which, parts),
        in_specs=[VMEM] * (len(sources) + 2),
        out_specs=[VMEM] * len(which),
        out_shape=[jax.ShapeDtypeStruct((size, begun.shape[1]), BF16)] * len(which),
        compiler_params=params(),
        name="spread",
    )(cells, *sources, begun)


def project_kernel(w_qkv, x, *refs):
    out = refs[-1]
    feature = x.shape[1]
    full = lax.dot_general(w_qkv[...], x[...], (((1,), (1,)), ((), ())), preferred_element_type=F32)
    scale = math.log2(math.e) / math.sqrt(HEAD)
    out[:feature] = full[:feature] * scale
    out[feature:] = full[feature:]


def project(w_qkv, x, *before):
    return pl.pallas_call(
        project_kernel,
        in_specs=[VMEM] * (2 + len(before)),
        out_specs=VMEM,
        out_shape=jax.ShapeDtypeStruct((w_qkv.shape[0], x.shape[0]), F32),
        compiler_params=params(),
        cost_estimate=cost(2 * w_qkv.size * x.shape[0], w_qkv.size),
        name="project",
    )(w_qkv, x, *before)


def merge_kernel(count, which, tile, *refs):
    x = refs[0]
    projected = refs[1 : count + 1]
    w_out, gain, w_up, w_down, out = refs[count + 1 :]
    feature = w_out.shape[0]
    for step in range(x.shape[0] // tile):
        rows = pl.ds(step * tile, tile)
        query = projected[which][:feature, rows].reshape(HEADS, HEAD, tile)
        scores = [
            jnp.sum(query * p[feature : 2 * feature, rows].reshape(HEADS, HEAD, tile), axis=1, keepdims=True)
            for p in projected
        ]
        top = functools.reduce(jnp.maximum, scores)
        weights = [jnp.exp2(s - top) for s in scores]
        inverse = 1.0 / functools.reduce(jnp.add, weights)
        mixture = functools.reduce(
            jnp.add,
            [
                (w * inverse) * p[2 * feature :, rows].reshape(HEADS, HEAD, tile)
                for w, p in zip(weights, projected)
            ],
        )
        mixture = mixture.reshape(feature, tile).astype(BF16)
        residual = x[rows, :].astype(F32) + lax.dot_general(
            mixture, w_out[...], (((0,), (0,)), ((), ())), preferred_element_type=F32
        )
        meansq = jnp.mean(residual * residual, axis=-1, keepdims=True)
        normed = (residual * lax.rsqrt(meansq + 1e-06) * gain[...]).astype(BF16)
        half = 0.5 * jnp.dot(normed, w_up[...], preferred_element_type=F32)
        hidden = (half + half * jnp.tanh(half)).astype(BF16)
        result = residual + jnp.dot(hidden, w_down[...], preferred_element_type=F32)
        out[rows, :] = result.astype(BF16)


def merge(x, projected, which, w_out, gain, w_up, w_down):
    size, feature = x.shape
    tile = math.gcd(size, 512)
    return pl.pallas_call(
        functools.partial(merge_kernel, len(projected), which, tile),
        in_specs=[VMEM] * (len(projected) + 5),
        out_specs=VMEM,
        out_shape=jax.ShapeDtypeStruct((size, feature), BF16),
        compiler_params=params(),
        cost_estimate=cost(8 * size * w_up.size, w_up.size),
        name="merge",
    )(x, *projected, w_out, gain, w_up, w_down)


def place_kernel(which, parts, *refs):
    pieces, out, sems = refs[: len(which)], refs[-2], refs[-1]
    size = pieces[0].shape[0]
    copies = []
    for slot, (k, piece) in enumerate(zip(which, pieces)):
        start = pl.multiple_of(part_of(k, parts) * size, size)
        copies.append(pltpu.make_async_copy(piece, out.at[pl.ds(start, size), :], sems.at[slot]))
        copies[-1].start()
    for copy in copies:
        copy.wait()


def place_parts(pieces, which, parts, *begun):
    size, feature = pieces[0].shape
    return pl.pallas_call(
        functools.partial(place_kernel, which, parts),
        in_specs=[VMEM] * len(pieces) + [HBM] * len(begun),
        out_specs=HBM,
        out_shape=jax.ShapeDtypeStruct((size * parts, feature), BF16),
        scratch_shapes=[pltpu.SemaphoreType.DMA((len(pieces),))],
        input_output_aliases={len(pieces): 0} if begun else {},
        compiler_params=params(),
        name="place",
    )(*vmem(*pieces), *begun)


def tiles_kernel(chunk, rows, cols, count, tiles, sources, own, out, total):
    step = pl.program_id(0)

    @pl.when(step == 0)
    def _():
        total[...] = own[...].astype(F32)

    for i in range(chunk):
        slot = step * chunk + i

        @pl.when(slot < count[0, 0])
        def _():
            start = pl.multiple_of(rows[0, slot] * TB, TB)
            total[pl.ds(start, TB), :] += jnp.dot(
                tiles[i], sources[cols[0, slot]], preferred_element_type=F32
            )

    @pl.when(step == pl.num_programs(0) - 1)
    def _():
        out[...] = total[...].astype(BF16)


def spread_tiles(rows, cols, count, tiles, sources, own):
    slots = tiles.shape[0]
    chunk = math.gcd(slots, 16)
    return pl.pallas_call(
        functools.partial(tiles_kernel, chunk),
        grid=(slots // chunk,),
        in_specs=[SMEM] * 3
        + [
            pl.BlockSpec((chunk, TB, TB), lambda s: (s, 0, 0)),
            pl.BlockSpec(sources.shape, lambda s: (0, 0, 0)),
            pl.BlockSpec(own.shape, lambda s: (0, 0)),
        ],
        out_specs=pl.BlockSpec(own.shape, lambda s: (0, 0)),
        out_shape=jax.ShapeDtypeStruct(own.shape, BF16),
        scratch_shapes=[pltpu.VMEM(own.shape, F32)],
        compiler_params=params(),
        name="tiles",
    )(rows, cols, count, tiles, sources, own)


def fetch_many(embeddings, need_ids, block_count):
    peer_count = lax.axis_size("node")
    feature = embeddings.shape[1]
    needed = need_ids[0]
    owners = needed // block_count
    within = needed % block_count
    peer_ids = jnp.arange(peer_count, dtype=jnp.int32)
    matches = owners[:, None] == peer_ids[None, :]
    request = jnp.sum(jnp.where(matches, within[:, None] + 1, 0), axis=0)
    swapped = request.reshape(-1, 2)[:, ::-1].reshape(-1)
    request_pair = jnp.stack([request, swapped], axis=1)
    incoming = lax.all_to_all(request_pair, "node", split_axis=0, concat_axis=0, tiled=True)
    parity = lax.axis_index("node") % 2
    own = embeddings.reshape(block_count, TB, feature)
    other = exchange(embeddings, "node", 1).reshape(block_count, TB, feature)
    stack = jnp.concatenate([own, other], axis=0)
    codes = jnp.where(incoming[:, 0] > 0, incoming[:, 0], block_count + incoming[:, 1])
    half = TB // 2
    halves = lax.dynamic_slice_in_dim(stack, parity * half, half, 1)
    chooser = (codes[:, None] - 1 == jnp.arange(2 * block_count, dtype=jnp.int32)[None, :]).astype(BF16)
    outgoing = jnp.einsum("pk,kid->pid", chooser, halves, preferred_element_type=F32).astype(BF16)
    arrived = lax.all_to_all(outgoing, "node", split_axis=0, concat_axis=0, tiled=True)
    return arrived.reshape(peer_count // 2, TB, feature)


def shards(
    embeddings,
    adjacency,
    tile_rows,
    tile_cols,
    tile_count,
    need_ids,
    w_query,
    w_key,
    w_value,
    w_out,
    mlp_gain,
    w_up,
    w_down,
):
    parts = lax.axis_size("beh")
    pairs = lax.axis_size("node") // 2
    block_count = embeddings.shape[0] // TB
    tiles = adjacency[0]
    if pairs * block_count <= tiles.shape[0]:
        far = range(pairs - 1, 0, -1)
        own, ids = load(embeddings, need_ids)
        asks = [exchange(need_ids if k == pairs - 1 else ids, "node", 2 * k) for k in far] + [ids]
        other = exchange(embeddings, "node", 1)
        served = serve(asks[:1], own, other, block_count, 10**10)
        *more, here = serve(asks[1:], own, other, block_count, 10**10)
        first, *rest = [exchange(block, "node", 2 * k) for k, block in zip(far, [*served, *more])]
        arrays = (tile_rows, tile_cols, tile_count, tiles)
        cells, begun = begin_spread(*arrays, [first, here], [pairs - 1, 0], own, pairs)
        last = spread_cells(cells, rest, begun, [parts - 1], parts)
        quarters = spread_cells(cells, rest, begun, list(range(parts - 1)), parts) + last
    else:
        sources = fetch_many(embeddings, need_ids, block_count)
        spread = spread_tiles(tile_rows, tile_cols, tile_count, tiles, sources, embeddings)
        size = spread.shape[0] // parts
        quarters = [lax.dynamic_slice_in_dim(spread, part_of(k, parts) * size, size, 0) for k in range(parts)]
    masks = beh_masks(parts)
    xs = [quarters[0]] + [exchange_beh(quarters[k], masks[k]) for k in range(1, parts)]
    w_qkv = jnp.concatenate([w_query, w_key, w_value], axis=1).T
    order = [parts - 1, *range(1, parts - 1), 0]
    projected = [project(w_qkv, xs[0])] * parts
    for k, before in zip(order[:-1], order[-1:] + order):
        projected[k] = project(w_qkv, xs[k], projected[before])
    merged = [merge(xs[k], projected, k, w_out, mlp_gain[None], w_up, w_down) for k in order]
    back = [exchange_beh(part, masks[k]) if k else part for k, part in zip(order, merged)]
    late = parts - 2
    begun = place_parts(back[:late] + back[late + 1 :], order[:late] + order[late + 1 :], parts)
    return place_parts(back[late : late + 1], order[late : late + 1], parts, begun)[None]


def solution(mesh):
    in_specs = (
        P("node", None),
        P("beh", "node", None, None),
        P("beh", "node"),
        P("beh", "node"),
        P("beh", "node"),
        P("beh", "node"),
        P(),
        P(),
        P(),
        P(),
        P(),
        P(),
        P(),
    )
    out_specs = P("beh", "node", None)
    return jax.shard_map(shards, mesh=mesh, in_specs=in_specs, out_specs=out_specs, check_vma=False)
```

```python
import functools
import math

import jax
import jax.numpy as jnp
from jax import lax
from jax.experimental import pallas as pl
from jax.experimental.pallas import tpu as pltpu
from jax.sharding import PartitionSpec as P

TB = 128
HEADS = 4
HEAD = 32
F32 = jnp.float32
BF16 = jnp.bfloat16
SMEM = pl.BlockSpec(memory_space=pltpu.SMEM)
VMEM = pl.BlockSpec(memory_space=pltpu.VMEM)
ANY = pl.BlockSpec(memory_space=pl.ANY)
HBM = pl.BlockSpec(memory_space=pltpu.HBM)
VMEM_LIMIT = 48 * 2**20


def hbm(*values):
    return [pltpu.with_memory_space_constraint(v, pltpu.HBM) for v in values]


def vmem(*values):
    return [pltpu.with_memory_space_constraint(v, pltpu.VMEM) for v in values]


def exchange(value, axis, mask):
    pairs = [(source, source ^ mask) for source in range(lax.axis_size(axis))]
    return lax.ppermute(value, axis, pairs)


def beh_masks(parts):
    first, *rest = range(parts - 1, 0, -1)
    return [(0, 0)] + list(zip(rest[::-1], rest)) + [(first, first)]


def exchange_beh(value, masks):
    peers = lax.axis_size("node")
    pairs = [
        (b * peers + n, (b ^ masks[n % 2]) * peers + n) for b in range(lax.axis_size("beh")) for n in range(peers)
    ]
    return lax.ppermute(value, ("beh", "node"), pairs)


def part_of(k, parts):
    even, odd = beh_masks(parts)[k]
    return lax.axis_index("beh") ^ jnp.where(lax.axis_index("node") % 2 == 0, even, odd)


def params(**more):
    return pltpu.CompilerParams(vmem_limit_bytes=VMEM_LIMIT, **more)


def cost(flops, moved):
    return pl.CostEstimate(flops=flops, bytes_accessed=moved, transcendentals=0)


def cells_kernel(chunk, pairs, columns, rows, cols, count, tiles, *refs):
    sources, refs = refs[: len(columns)], refs[len(columns) :]
    own, out, begun, total, held, row_list, col_list, sems = refs
    steps = tiles.shape[0] // chunk
    block_count = own.shape[0] // TB
    here = lax.axis_index("node") // 2
    lists = [
        pltpu.make_async_copy(source, target, sems.at[steps + k])
        for k, (source, target) in enumerate(((rows, row_list), (cols, col_list)))
    ]
    loads = [
        pltpu.make_async_copy(tiles.at[pl.ds(s * chunk, chunk)], held.at[s], sems.at[s]) for s in range(steps)
    ]
    for copy in lists:
        copy.start()
    for step, load in enumerate(loads):
        pl.when(step * chunk < count[0, 0])(load.start)
    total[...] = jnp.zeros_like(total)
    for copy in lists:
        copy.wait()
    for step, load in enumerate(loads):

        @pl.when(step * chunk < count[0, 0])
        def _():
            load.wait()
            for i in range(chunk):
                slot = step * chunk + i
                cell = row_list[0, slot] * pairs + (col_list[0, slot] ^ here)
                cell = jnp.where(slot < count[0, 0], cell, block_count * pairs)
                total[cell] += held[step, i].astype(F32)

    stack = jnp.concatenate([s[...] for s in sources], axis=0)
    others = [m for m in range(pairs) if m not in columns]
    for r in range(block_count):
        rows_of = pl.ds(r * TB, TB)
        lhs = jnp.concatenate([total[r * pairs + m].astype(BF16) for m in columns], axis=1)
        begun[rows_of, :] = own[rows_of, :].astype(F32) + jnp.dot(lhs, stack, preferred_element_type=F32)
        for k, m in enumerate(others):
            out[r * len(others) + k] = total[r * pairs + m].astype(BF16)


def begin_spread(rows, cols, count, tiles, sources, columns, own, pairs):
    slots = tiles.shape[0]
    chunk = math.gcd(slots, 16)
    block_count = own.shape[0] // TB
    return pl.pallas_call(
        functools.partial(cells_kernel, chunk, pairs, columns),
        in_specs=[HBM, HBM, SMEM, HBM] + [VMEM] * (len(sources) + 1),
        out_specs=[VMEM] * 2,
        out_shape=[
            jax.ShapeDtypeStruct((block_count * (pairs - len(columns)), TB, TB), BF16),
            jax.ShapeDtypeStruct(own.shape, F32),
        ],
        scratch_shapes=[
            pltpu.VMEM((block_count * pairs + 1, TB, TB), F32),
            pltpu.VMEM((slots // chunk, chunk, TB, TB), BF16),
            pltpu.SMEM(rows.shape, jnp.int32),
            pltpu.SMEM(cols.shape, jnp.int32),
            pltpu.SemaphoreType.DMA((slots // chunk + 2,)),
        ],
        compiler_params=params(),
        cost_estimate=cost(0, tiles.size * 2),
        name="cells",
    )(*hbm(rows, cols), count, *hbm(tiles), *sources, own)


def load_kernel(*refs):
    half = len(refs) // 2
    sems = refs[-1]
    copies = [pltpu.make_async_copy(refs[k], refs[half + k], sems.at[k]) for k in range(half)]
    for copy in copies:
        copy.start()
    for copy in copies:
        copy.wait()


def load(*sources):
    return pl.pallas_call(
        load_kernel,
        in_specs=[HBM] * len(sources),
        out_specs=[VMEM] * len(sources),
        out_shape=[jax.ShapeDtypeStruct(s.shape, s.dtype) for s in sources],
        scratch_shapes=[pltpu.SemaphoreType.DMA((len(sources),))],
        compiler_params=params(),
        cost_estimate=cost(0, sum(s.size * 2 for s in sources)),
        name="load",
    )(*hbm(*sources))


def serve_kernel(block_count, pairs, *refs):
    asks, (own, other), outs = refs[:pairs], refs[pairs : pairs + 2], refs[pairs + 2 :]
    here = lax.axis_index("node") // 2
    core = lax.axis_index("node") % 2
    blocks = []
    for ask in asks:
        lanes = lax.broadcasted_iota(jnp.int32, ask.shape, 1)
        blocks.append(jnp.sum(jnp.where(lanes == here, ask[...], 0)) - 2 * here * block_count)
    for block, out in zip(blocks, outs):
        upper = (block >= block_count).astype(jnp.int32)
        start = pl.multiple_of((block - upper * block_count) * TB, TB)

        @pl.when(upper == core)
        def _():
            out[...] = own[pl.ds(start, TB), :]

        @pl.when(upper != core)
        def _():
            out[...] = other[pl.ds(start, TB), :]


def serve(asks, own, other, block_count, weight):
    pairs = len(asks)
    return pl.pallas_call(
        functools.partial(serve_kernel, block_count, pairs),
        in_specs=[VMEM] * (pairs + 2),
        out_specs=[VMEM] * pairs,
        out_shape=[jax.ShapeDtypeStruct((TB, own.shape[1]), own.dtype)] * pairs,
        compiler_params=params(),
        cost_estimate=cost(weight, own.size),
        name="serve",
    )(*asks, own, other)


def spread_kernel(columns, which, parts, cells, *refs):
    sources, begun, outs = refs[:columns], refs[columns], refs[columns + 1 :]
    stack = jnp.concatenate([s[...] for s in sources[::-1]], axis=0)
    size = outs[0].shape[0]
    for k, out in zip(which, outs):
        part = part_of(k, parts)
        start = pl.multiple_of(part * size, size)
        block = part * (size // TB)
        for r in range(size // TB):
            lhs = jnp.concatenate([cells[(block + r) * columns + m] for m in range(columns)], axis=1)
            total = jnp.dot(lhs, stack, preferred_element_type=F32)
            out[r * TB : (r + 1) * TB, :] = (begun[pl.ds(start + r * TB, TB), :] + total).astype(BF16)


def spread_cells(cells, sources, begun, which, parts):
    size = begun.shape[0] // parts
    return pl.pallas_call(
        functools.partial(spread_kernel, len(sources), which, parts),
        in_specs=[VMEM] * (len(sources) + 2),
        out_specs=[VMEM] * len(which),
        out_shape=[jax.ShapeDtypeStruct((size, begun.shape[1]), BF16)] * len(which),
        compiler_params=params(),
        name="spread",
    )(cells, *sources, begun)


def project_kernel(w_qkv, x, *refs):
    out = refs[-1]
    feature = x.shape[1]
    full = lax.dot_general(w_qkv[...], x[...], (((1,), (1,)), ((), ())), preferred_element_type=F32)
    scale = math.log2(math.e) / math.sqrt(HEAD)
    out[:feature] = full[:feature] * scale
    out[feature:] = full[feature:]


def project(w_qkv, x, *before):
    return pl.pallas_call(
        project_kernel,
        in_specs=[VMEM] * (2 + len(before)),
        out_specs=VMEM,
        out_shape=jax.ShapeDtypeStruct((w_qkv.shape[0], x.shape[0]), F32),
        compiler_params=params(),
        cost_estimate=cost(2 * w_qkv.size * x.shape[0], w_qkv.size),
        name="project",
    )(w_qkv, x, *before)


def merge_kernel(count, which, tile, *refs):
    x = refs[0]
    projected = refs[1 : count + 1]
    w_out, gain, w_up, w_down, out = refs[count + 1 :]
    feature = w_out.shape[0]
    for step in range(x.shape[0] // tile):
        rows = pl.ds(step * tile, tile)
        query = projected[which][:feature, rows].reshape(HEADS, HEAD, tile)
        scores = [
            jnp.sum(query * p[feature : 2 * feature, rows].reshape(HEADS, HEAD, tile), axis=1, keepdims=True)
            for p in projected
        ]
        top = functools.reduce(jnp.maximum, scores)
        weights = [jnp.exp2(s - top) for s in scores]
        inverse = 1.0 / functools.reduce(jnp.add, weights)
        mixture = functools.reduce(
            jnp.add,
            [
                (w * inverse) * p[2 * feature :, rows].reshape(HEADS, HEAD, tile)
                for w, p in zip(weights, projected)
            ],
        )
        mixture = mixture.reshape(feature, tile).astype(BF16)
        residual = x[rows, :].astype(F32) + lax.dot_general(
            mixture, w_out[...], (((0,), (0,)), ((), ())), preferred_element_type=F32
        )
        meansq = jnp.mean(residual * residual, axis=-1, keepdims=True)
        normed = (residual * lax.rsqrt(meansq + 1e-06) * gain[...]).astype(BF16)
        half = 0.5 * jnp.dot(normed, w_up[...], preferred_element_type=F32)
        hidden = (half + half * jnp.tanh(half)).astype(BF16)
        result = residual + jnp.dot(hidden, w_down[...], preferred_element_type=F32)
        out[rows, :] = result.astype(BF16)


def merge(x, projected, which, w_out, gain, w_up, w_down):
    size, feature = x.shape
    tile = math.gcd(size, 512)
    return pl.pallas_call(
        functools.partial(merge_kernel, len(projected), which, tile),
        in_specs=[VMEM] * (len(projected) + 5),
        out_specs=VMEM,
        out_shape=jax.ShapeDtypeStruct((size, feature), BF16),
        compiler_params=params(),
        cost_estimate=cost(8 * size * w_up.size, w_up.size),
        name="merge",
    )(x, *projected, w_out, gain, w_up, w_down)


def place_kernel(which, parts, *refs):
    pieces, out, sems = refs[: len(which)], refs[-2], refs[-1]
    size = pieces[0].shape[0]
    copies = []
    for slot, (k, piece) in enumerate(zip(which, pieces)):
        start = pl.multiple_of(part_of(k, parts) * size, size)
        copies.append(pltpu.make_async_copy(piece, out.at[pl.ds(start, size), :], sems.at[slot]))
        copies[-1].start()
    for copy in copies:
        copy.wait()


def place_parts(pieces, which, parts, *begun):
    size, feature = pieces[0].shape
    return pl.pallas_call(
        functools.partial(place_kernel, which, parts),
        in_specs=[VMEM] * len(pieces) + [HBM] * len(begun),
        out_specs=HBM,
        out_shape=jax.ShapeDtypeStruct((size * parts, feature), BF16),
        scratch_shapes=[pltpu.SemaphoreType.DMA((len(pieces),))],
        input_output_aliases={len(pieces): 0} if begun else {},
        compiler_params=params(),
        name="place",
    )(*vmem(*pieces), *begun)


def tiles_kernel(chunk, rows, cols, count, tiles, sources, own, out, total):
    step = pl.program_id(0)

    @pl.when(step == 0)
    def _():
        total[...] = own[...].astype(F32)

    for i in range(chunk):
        slot = step * chunk + i

        @pl.when(slot < count[0, 0])
        def _():
            start = pl.multiple_of(rows[0, slot] * TB, TB)
            total[pl.ds(start, TB), :] += jnp.dot(
                tiles[i], sources[cols[0, slot]], preferred_element_type=F32
            )

    @pl.when(step == pl.num_programs(0) - 1)
    def _():
        out[...] = total[...].astype(BF16)


def spread_tiles(rows, cols, count, tiles, sources, own):
    slots = tiles.shape[0]
    chunk = math.gcd(slots, 16)
    return pl.pallas_call(
        functools.partial(tiles_kernel, chunk),
        grid=(slots // chunk,),
        in_specs=[SMEM] * 3
        + [
            pl.BlockSpec((chunk, TB, TB), lambda s: (s, 0, 0)),
            pl.BlockSpec(sources.shape, lambda s: (0, 0, 0)),
            pl.BlockSpec(own.shape, lambda s: (0, 0)),
        ],
        out_specs=pl.BlockSpec(own.shape, lambda s: (0, 0)),
        out_shape=jax.ShapeDtypeStruct(own.shape, BF16),
        scratch_shapes=[pltpu.VMEM(own.shape, F32)],
        compiler_params=params(),
        name="tiles",
    )(rows, cols, count, tiles, sources, own)


def fetch_many(embeddings, need_ids, block_count):
    peer_count = lax.axis_size("node")
    feature = embeddings.shape[1]
    needed = need_ids[0]
    owners = needed // block_count
    within = needed % block_count
    peer_ids = jnp.arange(peer_count, dtype=jnp.int32)
    matches = owners[:, None] == peer_ids[None, :]
    request = jnp.sum(jnp.where(matches, within[:, None] + 1, 0), axis=0)
    swapped = request.reshape(-1, 2)[:, ::-1].reshape(-1)
    request_pair = jnp.stack([request, swapped], axis=1)
    incoming = lax.all_to_all(request_pair, "node", split_axis=0, concat_axis=0, tiled=True)
    parity = lax.axis_index("node") % 2
    own = embeddings.reshape(block_count, TB, feature)
    other = exchange(embeddings, "node", 1).reshape(block_count, TB, feature)
    stack = jnp.concatenate([own, other], axis=0)
    codes = jnp.where(incoming[:, 0] > 0, incoming[:, 0], block_count + incoming[:, 1])
    half = TB // 2
    halves = lax.dynamic_slice_in_dim(stack, parity * half, half, 1)
    chooser = (codes[:, None] - 1 == jnp.arange(2 * block_count, dtype=jnp.int32)[None, :]).astype(BF16)
    outgoing = jnp.einsum("pk,kid->pid", chooser, halves, preferred_element_type=F32).astype(BF16)
    arrived = lax.all_to_all(outgoing, "node", split_axis=0, concat_axis=0, tiled=True)
    return arrived.reshape(peer_count // 2, TB, feature)


def shards(
    embeddings,
    adjacency,
    tile_rows,
    tile_cols,
    tile_count,
    need_ids,
    w_query,
    w_key,
    w_value,
    w_out,
    mlp_gain,
    w_up,
    w_down,
):
    parts = lax.axis_size("beh")
    pairs = lax.axis_size("node") // 2
    block_count = embeddings.shape[0] // TB
    tiles = adjacency[0]
    if pairs * block_count <= tiles.shape[0]:
        far = range(pairs - 1, 0, -1)
        own, ids = load(embeddings, need_ids)
        asks = [exchange(need_ids if k == pairs - 1 else ids, "node", 2 * k) for k in far] + [ids]
        other = exchange(embeddings, "node", 1)
        served = serve(asks[:1], own, other, block_count, 10**10)
        *more, here = serve(asks[1:], own, other, block_count, 10**10)
        first, *rest = [exchange(block, "node", 2 * k) for k, block in zip(far, [*served, *more])]
        arrays = (tile_rows, tile_cols, tile_count, tiles)
        cells, begun = begin_spread(*arrays, [first, here], [pairs - 1, 0], own, pairs)
        last = spread_cells(cells, rest, begun, [parts - 1], parts)
        quarters = spread_cells(cells, rest, begun, list(range(parts - 1)), parts) + last
    else:
        sources = fetch_many(embeddings, need_ids, block_count)
        spread = spread_tiles(tile_rows, tile_cols, tile_count, tiles, sources, embeddings)
        size = spread.shape[0] // parts
        quarters = [lax.dynamic_slice_in_dim(spread, part_of(k, parts) * size, size, 0) for k in range(parts)]
    masks = beh_masks(parts)
    xs = [quarters[0]] + [exchange_beh(quarters[k], masks[k]) for k in range(1, parts)]
    w_qkv = jnp.concatenate([w_query, w_key, w_value], axis=1).T
    order = [parts - 1, *range(1, parts - 1), 0]
    projected = [project(w_qkv, xs[0])] * parts
    for k, before in zip(order[:-1], order[-1:] + order):
        projected[k] = project(w_qkv, xs[k], projected[before])
    merged = [merge(xs[k], projected, k, w_out, mlp_gain[None], w_up, w_down) for k in order]
    back = [exchange_beh(part, masks[k]) if k else part for k, part in zip(order, merged)]
    late = parts - 2
    begun = place_parts(back[:late] + back[late + 1 :], order[:late] + order[late + 1 :], parts)
    return place_parts(back[late : late + 1], order[late : late + 1], parts, begun)[None]


def solution(mesh):
    in_specs = (
        P("node", None),
        P("beh", "node", None, None),
        P("beh", "node"),
        P("beh", "node"),
        P("beh", "node"),
        P("beh", "node"),
        P(),
        P(),
        P(),
        P(),
        P(),
        P(),
        P(),
    )
    out_specs = P("beh", "node", None)
    return jax.shard_map(shards, mesh=mesh, in_specs=in_specs, out_specs=out_specs, check_vma=False)
```
